256 devices in a mesh: group: 16 (over x, y_hi, core), dp: 16 (over y_lo, z).
Axes of the slice: x: 4, y: 4 (y_hi: 2, y_lo: 2; y = y_hi * 2 + y_lo), z: 8, core: 2. Of those that a mesh axis runs over, the one named last changes fastest.
Arguments:
- student: bfloat16 [32768, 1024], P(('group', 'dp')), may hold values from -6 to 6
- teacher: bfloat16 [32768, 4096], P(('group', 'dp')), may hold values from -6 to 6
- teacher_similarity: float32 [32768, 2048], P(('group', 'dp')), may hold values from -0.5 to 1, as said below
- projector: bfloat16 [1024, 4096], replicated, may hold values from -0.1875 to 0.1875
- hard_group: int32 [32768, 2], P(('group', 'dp')), may hold values from 0 to 15, all different within a row; in each aligned block of 128 rows (0 to 127, 128 to 255, ...) at most 24 rows name the same one
- hard_local: int32 [32768, 2], P(('group', 'dp')), may hold values from 0 to 127
- hard_count: int32 [32768], P(('group', 'dp')), may hold values from 1 to 2
- text_weight: float32 [32768], P(('group', 'dp')), may hold values from 0.5 to 13
Outputs:
- mean_loss: float32 [], replicated
- student_gradient: bfloat16 [32768, 1024], P(('group', 'dp'))
- projector_gradient: float32 [1024, 4096], P('group', 'dp')
The draws below stay inside these ranges and needn't reach their ends.
Inputs may be any that keep to these rules, and one draw needn't show every extreme that they name: `hard_group`: A text's 2 entries name different groups. Among the 128 texts of one device (aligned blocks of 128 rows) no group is named more than 24 times, and some block names some group exactly 24 times. Symmetric inside each similarity set: for the set starting at text s, teacher_similarity[i, j - s] equals teacher_similarity[j, i - s]; a text's entry for itself is 1.
All inputs are finite; a program needn't handle non-finite values.
Results may differ from the reference program's by a relative error of at most 0.025.
Values may be sent and summed in bfloat16 or wider, within the bound.
A program may use at most 192 MiB of HBM per device.

```python
import math
import jax
import jax.numpy as jnp
import numpy as np
from jax import lax

DS = 1024
DP = 4096
ROWS = 128
HARD = 2
SET_ROWS = 2048
TEXTS = 32768
SLOTS = 24
N_GROUP = 16
N_DP = 16


def draw_text_weight(key, part):
    key = jax.random.fold_in(key, 7)
    ramp = jnp.arange(TEXTS, dtype=jnp.float32) / (TEXTS - 1)
    rough = jax.random.uniform(key, (TEXTS,), jnp.float32, 0.7, 1.3)
    return (1.0 + 4.0 * ramp) * rough


def draw_teacher_similarity(key, part):
    key = jax.random.fold_in(key, 11)
    first = jax.random.fold_in(key, 0)
    shape = (N_GROUP, SET_ROWS, SET_ROWS)
    base = jax.random.uniform(first, shape, jnp.float32, -0.2, 0.9)
    paired = 0.5 * (base + jnp.swapaxes(base, 1, 2))
    diagonal_mask = jnp.eye(SET_ROWS, dtype=jnp.bool_)
    paired = jnp.where(diagonal_mask[None, :, :], 1.0, paired)
    return paired.reshape(TEXTS, SET_ROWS)


def with_ends(entries, own_key, least, high):
    dims = entries.shape
    place = [jax.random.randint(jax.random.fold_in(own_key, axis), (), 0, dims[axis]) for axis in range(len(dims))]
    entries = entries.at[tuple(place)].set(least)
    longest = dims.index(max(dims))
    place[longest] = (place[longest] + 1) % dims[longest]
    return entries.at[tuple(place)].set(high)


def block_levels(own_key, shape, cuts, low, high):
    gain = 1.0
    for axis_at, blocks in cuts:
        draws = jax.random.uniform(jax.random.fold_in(jax.random.fold_in(own_key, 6), axis_at), (blocks,), jnp.float32, low / len(cuts), high / len(cuts))
        gain = gain * jnp.repeat(jnp.exp(draws), shape[axis_at] // blocks).reshape((-1,) + (1,) * (len(shape) - 1 - axis_at))
    return gain


def routed_block(rng, own, number, rows, amount, top, limit, lean):
    sequence = jax.random.permutation(rng, amount)
    packed, common = portions_of(amount, rows * top, limit, lean, True), portions_of(amount, rows * top, limit, lean, False)
    places = jnp.arange(amount)

    def named(lengths, rotation):
        used = int((lengths > 0).sum())
        fixed = max(1, used // 4)
        moved = fixed + (places - fixed + rotation * (used - fixed)) % max(1, amount - fixed)
        return jnp.zeros((amount,), jnp.int32).at[sequence[jnp.where(places < fixed, places, moved)]].set(jnp.asarray(lengths, jnp.int32))

    lengths = jnp.where(number % 4 == 0, named(packed, number // 4), named(common, number - number // 4 - 1))
    mixed = jax.random.permutation(jax.random.fold_in(own, 3), amount)
    giver, taker = mixed[0:amount // 2 * 2:2], mixed[1:amount // 2 * 2:2]
    room = jnp.minimum(lengths[giver] - 1, limit - lengths[taker]) // 2
    room = jnp.where((giver == sequence[0]) | (taker == sequence[0]) | (lengths[taker] == 0), 0, jnp.maximum(room, 0))
    moved = jax.random.randint(jax.random.fold_in(own, 4), (amount // 2,), 0, 1 << 20) % (room + 1)
    lengths = lengths.at[giver].add(-moved).at[taker].add(moved)
    items = jnp.searchsorted(jnp.cumsum(lengths), jnp.arange(rows * top), side="right").astype(jnp.int32)
    listing = items.reshape(top, rows).T
    listing = listing[jax.random.permutation(jax.random.fold_in(own, 1), rows)]
    rotation = jax.random.randint(jax.random.fold_in(own, 2), (rows, 1), 0, top)
    return jnp.take_along_axis(listing, (jnp.arange(top)[None, :] + rotation) % top, axis=1)


def portions_of(count, total, bound, lean, full):
    loads = [(1 << 20) // math.isqrt(standing ** lean) + 1 for standing in range(1, count + 1)]
    largest = bound if full else min(bound, max(-(-total // count), total * loads[0] // sum(loads)))
    least = 1 if total - largest >= count - 1 else 0
    counts, surplus = [largest] + [least] * (count - 1), total - largest - least * (count - 1)
    while surplus > 0:
        free = [i for i in range(1, count) if counts[i] < largest] or [i for i in range(1, count) if counts[i] < bound]
        pool, budget = sum([loads[i] for i in free]), surplus
        for i in free:
            more = min(bound - counts[i], max(1, budget * loads[i] // pool), surplus)
            counts[i] = counts[i] + more
            surplus = surplus - more
    return np.array(counts)


def normal_values(own_key, shape, spread, most, cuts=(), kind=jnp.bfloat16):
    loudness = block_levels(own_key, shape, cuts, -0.22, 0.18) if cuts else 1.0
    values = jax.random.normal(own_key, shape, jnp.float32) * spread * loudness
    return jnp.minimum(jnp.maximum(values, -most), most).astype(kind)


def setup_inputs(seed: int = 0) -> dict:
    splits = jax.random.split(jax.random.key(seed), 9)
    student = normal_values(splits[0], (TEXTS, DS), 1.0, 6.0, ((0, 256),))
    teacher = normal_values(splits[1], (TEXTS, DP), 1.0, 6.0, ((0, 256),))
    teacher_similarity = draw_teacher_similarity(jax.random.fold_in(splits[8], 71), 0)
    projector = normal_values(splits[3], (DS, DP), DS ** -0.5, 0.1875)
    hard_group_keys = jax.random.split(jax.random.fold_in(splits[4], 1), TEXTS // ROWS)
    hard_group_turns = jax.random.permutation(jax.random.fold_in(splits[4], 3), TEXTS // ROWS)
    hard_group = jax.vmap(lambda own, number: routed_block(jax.random.fold_in(splits[4], 2), own, number, ROWS, N_GROUP, HARD, SLOTS, 2))(hard_group_keys, hard_group_turns).reshape((TEXTS, HARD))
    hard_local = with_ends(jax.random.randint(splits[5], (TEXTS, HARD), 0, ROWS), jax.random.fold_in(splits[5], 1), 0, ROWS - 1).astype(jnp.int32)
    hard_count = with_ends(jax.random.randint(splits[6], (TEXTS,), 1, HARD + 1), jax.random.fold_in(splits[6], 1), 1, HARD).astype(jnp.int32)
    text_weight = draw_text_weight(jax.random.fold_in(splits[8], 71), 0)
    return {"student": student, "teacher": teacher, "teacher_similarity": teacher_similarity, "projector": projector, "hard_group": hard_group, "hard_local": hard_local, "hard_count": hard_count, "text_weight": text_weight}


EPSILON = 1e-06
SOFTMAX_TEMP = 0.05
SIMILARITY_COEF = 200.0
HARD_WEIGHT = 20.0
LOSS_SCALE = 1024.0

def unit_rows_of(values):
    norm_values = jnp.sqrt(lax.optimization_barrier(jnp.sum(values * values, 1, keepdims=True)) + EPSILON)
    return (values / norm_values, norm_values)

def group_part(triple):
    unit_block, teacher_similarity, weight_block = triple
    student_similarity = jnp.dot(unit_block, unit_block.T, preferred_element_type=jnp.float32)
    element_count = student_similarity.shape[0]
    off_diagonal = 1.0 - jnp.eye(element_count, dtype=jnp.float32)
    student_scaled = student_similarity / SOFTMAX_TEMP
    teacher_scaled = teacher_similarity / SOFTMAX_TEMP
    student_exp = jnp.exp(student_scaled) * off_diagonal
    teacher_exp = jnp.exp(teacher_scaled) * off_diagonal
    total_s = lax.optimization_barrier(jnp.sum(student_exp, 1))
    total_t = lax.optimization_barrier(jnp.sum(teacher_exp, 1))
    log_s = jnp.log(total_s)
    log_t = jnp.log(total_t)
    student_probability = student_exp / total_s[:, None]
    teacher_probability = teacher_exp / total_t[:, None]
    sim_difference = student_similarity - teacher_similarity
    sim_term = SIMILARITY_COEF / element_count * lax.optimization_barrier(jnp.sum(sim_difference * sim_difference, 1))
    kl_term = lax.optimization_barrier(jnp.sum(teacher_probability * (teacher_scaled - log_t[:, None] - (student_scaled - log_s[:, None])), 1))
    device_routine = weight_block[:, None] * (2.0 * SIMILARITY_COEF / element_count * sim_difference + (student_probability - teacher_probability) / SOFTMAX_TEMP)
    pair_weight = (device_routine + device_routine.T).astype(jnp.bfloat16)
    set_grad = jnp.dot(pair_weight, unit_block, preferred_element_type=jnp.float32)
    return (set_grad, sim_term + kl_term)

def reference(student, teacher, teacher_similarity, projector, hard_group, hard_local, hard_count, text_weight):
    projected = jnp.dot(student, projector, preferred_element_type=jnp.float32)
    unit_float, norm_values = unit_rows_of(projected)
    student_unit = unit_float.astype(jnp.bfloat16)
    teacher_float, teacher_norm = unit_rows_of(teacher.astype(jnp.float32))
    teacher_unit = teacher_float.astype(jnp.bfloat16)
    set_grad, set_terms = lax.map(group_part, (student_unit.reshape(N_GROUP, SET_ROWS, DP), teacher_similarity.reshape(N_GROUP, SET_ROWS, SET_ROWS), text_weight.reshape(N_GROUP, SET_ROWS)))
    set_grad = set_grad.reshape(TEXTS, DP)
    set_terms = set_terms.reshape(TEXTS)
    row_ids = jnp.arange(TEXTS, dtype=jnp.int32)
    column_ids = row_ids // ROWS % N_DP
    target = ((hard_group * N_DP + column_ids[:, None]) * ROWS + hard_local).astype(jnp.int32)
    neg_unit = student_unit[target].astype(jnp.float32)
    neg_teacher = teacher_unit[target].astype(jnp.float32)
    query_unit = student_unit.astype(jnp.float32)
    query_teacher = teacher_unit.astype(jnp.float32)
    student_hard = jnp.einsum('nd,nkd->nk', query_unit, neg_unit)
    teacher_hard = jnp.einsum('nd,nkd->nk', query_teacher, neg_teacher)
    validity = (jnp.arange(HARD, dtype=jnp.int32)[None, :] < hard_count[:, None]).astype(jnp.float32)
    weight = validity * HARD_WEIGHT / hard_count[:, None].astype(jnp.float32)
    hard_gap = student_hard - teacher_hard
    hard_term = lax.optimization_barrier(jnp.sum(weight * hard_gap * hard_gap, 1))
    factor = 2.0 * text_weight[:, None] * weight * hard_gap
    own_hard = jnp.einsum('nk,nkd->nd', factor, neg_unit)
    returned = (factor[:, :, None] * query_unit[:, None, :]).astype(jnp.bfloat16)
    remote = jnp.zeros((TEXTS, DP), jnp.float32).at[target.reshape(-1)].add(returned.reshape(TEXTS * HARD, DP).astype(jnp.float32))
    cos_term = 1.0 - lax.optimization_barrier(jnp.sum(query_unit * query_teacher, 1))
    mean_loss = jnp.sum(text_weight * (cos_term + set_terms + hard_term)) / TEXTS
    unit_gradient = LOSS_SCALE * (set_grad - text_weight[:, None] * query_teacher + own_hard + remote)
    inner = lax.optimization_barrier(jnp.sum(projected * unit_gradient, 1, keepdims=True))
    proj_gradient = (unit_gradient / norm_values - projected * inner / (norm_values * norm_values * norm_values)).astype(jnp.bfloat16)
    student_gradient = jnp.dot(proj_gradient, projector.T, preferred_element_type=jnp.float32).astype(jnp.bfloat16)
    blocks = TEXTS // ROWS

    def add_block(carry, pieces):
        text_block, grad_block = pieces
        term = jnp.dot(text_block.T, grad_block, preferred_element_type=jnp.float32).astype(jnp.bfloat16)
        term = lax.optimization_barrier(term)
        return (carry + term.astype(jnp.float32), None)
    projector_gradient, unused = lax.scan(add_block, jnp.zeros((DS, DP), jnp.float32), (student.reshape(blocks, ROWS, DS), proj_gradient.reshape(blocks, ROWS, DP)))
    return (mean_loss, student_gradient, projector_gradient)
```

```python
import jax
import jax.numpy as jnp
from jax import lax
from jax.sharding import PartitionSpec as P

HARD = 2
EPSILON = 1e-06
SOFTMAX_TEMP = 0.05
SIMILARITY_COEF = 200.0
HARD_WEIGHT = 20.0
LOSS_SCALE = 1024.0


def row_norms(values):
    return jnp.sqrt(jnp.sum(values * values, 1, keepdims=True) + EPSILON)


def dot_t(left, right):
    return lax.dot_general(
        left, right, (((1,), (1,)), ((), ())), preferred_element_type=jnp.float32
    )


def two_part_dot_t(left, right):
    high = left.astype(jnp.bfloat16)
    low = (left - high.astype(jnp.float32)).astype(jnp.bfloat16)
    both = dot_t(jnp.concatenate([high, low], 0), right)
    rows = left.shape[0]
    return both[:rows] + both[rows:]


def local(
    student, teacher, teacher_similarity, projector, hard_group, hard_local, hard_count, text_weight
):
    rows = student.shape[0]
    groups = lax.axis_size("group")
    columns = lax.axis_size("dp")
    set_count = rows * columns
    position = lax.axis_index("dp")
    my_group = lax.axis_index("group")
    student_set = lax.all_gather(student, "dp", axis=0, tiled=True)
    student_col = lax.all_gather(student, "group", axis=0, tiled=True)
    teacher_float = teacher.astype(jnp.float32)
    teacher_unit = (teacher_float / row_norms(teacher_float)).astype(jnp.bfloat16)
    teacher_cols = lax.all_to_all(teacher_unit, "group", split_axis=1, concat_axis=0, tiled=True)
    projected = jnp.dot(student, projector, preferred_element_type=jnp.float32)
    norm = row_norms(projected)
    cosine = jnp.sum(projected * teacher_unit.astype(jnp.float32), 1, keepdims=True)
    back = dot_t(projected.astype(jnp.bfloat16), projector)
    target = (hard_group * rows + hard_local).astype(jnp.float32)
    order = jnp.arange(HARD, dtype=jnp.int32)[None, :]
    count = hard_count[:, None]
    entry_weight = (
        (order < count).astype(jnp.float32) * HARD_WEIGHT / count.astype(jnp.float32)
    ) * text_weight[:, None]
    own_index = position * rows + jnp.arange(rows, dtype=jnp.int32)
    off_diagonal = jnp.arange(set_count, dtype=jnp.int32)[None, :] != own_index[:, None]
    teacher_scaled = teacher_similarity / SOFTMAX_TEMP
    teacher_exp = jnp.where(off_diagonal, jnp.exp(teacher_scaled), 0.0)
    total_t = jnp.sum(teacher_exp, 1, keepdims=True)
    facts = jnp.concatenate(
        [norm, 1.0 / total_t, text_weight[:, None], target, entry_weight], 1
    ).T
    facts_set = lax.all_gather(facts[:3], "dp", axis=1, tiled=True)
    facts_col = lax.all_gather(facts, "group", axis=1, tiled=True)

    gram = dot_t(teacher_cols, teacher_cols)
    ids = jnp.arange(groups * rows, dtype=jnp.int32).astype(jnp.float32)
    part = jnp.stack(
        [jnp.sum(jnp.where(ids[:, None] == facts_col[3 + k][None, :], gram, 0.0), 0) for k in range(HARD)]
    )
    teacher_hard = lax.psum(part, "group")

    norm_set, total_t_set, weight_set = facts_set[0][None], facts_set[1][None], facts_set[2][None]
    similarity = two_part_dot_t(back / norm, student_set) / norm_set
    student_exp = jnp.where(off_diagonal, jnp.exp(similarity / SOFTMAX_TEMP), 0.0)
    total_s = jnp.sum(student_exp, 1, keepdims=True)
    total_s_set = lax.all_gather((1.0 / total_s)[:, 0], "dp", axis=0, tiled=True)[None]
    gap = similarity - teacher_similarity
    weight = text_weight[:, None]
    sim_term = SIMILARITY_COEF / set_count * jnp.sum(gap * gap, 1, keepdims=True)
    kl_term = (
        jnp.sum(teacher_exp * gap, 1, keepdims=True) * (-1.0 / SOFTMAX_TEMP) / total_t
        + jnp.log(total_s)
        - jnp.log(total_t)
    )
    pair = (2.0 * SIMILARITY_COEF / set_count) * gap * (weight + weight_set) + (
        student_exp * (weight / total_s + weight_set * total_s_set)
        - teacher_exp * (weight / total_t + weight_set * total_t_set)
    ) / SOFTMAX_TEMP
    set_part = jnp.dot(
        (pair / norm_set).astype(jnp.bfloat16), student_set, preferred_element_type=jnp.float32
    )

    norm_col = facts_col[0][None]
    cross = two_part_dot_t(back / norm, student_col) / norm_col
    own_hard = lax.dynamic_slice_in_dim(teacher_hard, my_group * rows, rows, 1)
    own_ids = (my_group * rows + jnp.arange(rows, dtype=jnp.int32)).astype(jnp.float32)[:, None]
    hard = jnp.zeros_like(cross)
    hard_loss = 0.0
    for k in range(HARD):
        asked = jnp.where(ids[None, :] == target[:, k : k + 1], entry_weight[:, k : k + 1], 0.0)
        difference = cross - own_hard[k][:, None]
        hard = hard + asked * difference
        hard_loss = hard_loss + jnp.sum(asked * difference * difference)
        listed = jnp.where(facts_col[3 + k][None] == own_ids, facts_col[5 + k][None], 0.0)
        hard = hard + listed * (cross - teacher_hard[k][None])
    hard_part = jnp.dot(
        (2.0 * hard / norm_col).astype(jnp.bfloat16),
        student_col,
        preferred_element_type=jnp.float32,
    )
    local_loss = jnp.sum(weight * (1.0 - cosine / norm + sim_term + kl_term)) + hard_loss
    mean_loss = lax.psum(local_loss, ("group", "dp")) / (rows * groups * columns)

    combined = LOSS_SCALE * (set_part + hard_part)
    inner = jnp.sum(back * combined, 1, keepdims=True) - LOSS_SCALE * weight * cosine
    inside = combined / norm - student.astype(jnp.float32) * (inner / (norm * norm * norm))
    high = inside.astype(jnp.bfloat16)
    low = (inside - high.astype(jnp.float32)).astype(jnp.bfloat16)
    both = jnp.dot(
        jnp.concatenate([high, low], 0), projector, preferred_element_type=jnp.float32
    )
    proj_gradient = (
        both[:rows]
        + both[rows:]
        - (LOSS_SCALE * weight / norm) * teacher_unit.astype(jnp.float32)
    ).astype(jnp.bfloat16)
    student_gradient = dot_t(proj_gradient, projector).astype(jnp.bfloat16)
    gradient_cols = lax.all_to_all(proj_gradient, "dp", split_axis=1, concat_axis=0, tiled=True)
    within = lax.dot_general(
        student_set, gradient_cols, (((0,), (0,)), ((), ())), preferred_element_type=jnp.float32
    ).astype(jnp.bfloat16)
    projector_gradient = lax.psum_scatter(within, "group", scatter_dimension=0, tiled=True).astype(
        jnp.float32
    )
    return (mean_loss, student_gradient, projector_gradient)


def solution(mesh):
    return jax.shard_map(
        local,
        mesh=mesh,
        in_specs=(
            P(("group", "dp"), None),
            P(("group", "dp"), None),
            P(("group", "dp"), None),
            P(),
            P(("group", "dp"), None),
            P(("group", "dp"), None),
            P(("group", "dp")),
            P(("group", "dp")),
        ),
        out_specs=(P(), P(("group", "dp"), None), P("group", "dp")),
        check_vma=False,
    )
```

```python
import functools
import jax
import jax.numpy as jnp
from jax import lax
from jax.experimental import pallas as pl
from jax.experimental.pallas import tpu as pltpu
from jax.sharding import PartitionSpec as P

HARD = 2
EPSILON = 1e-06
INVERSE_TEMP = 20.0
SIMILARITY_COEF = 200.0
HARD_WEIGHT = 20.0
LOSS_SCALE = 1024.0
MESH = pl.DeviceIdType.MESH
F32 = jnp.float32
BF16 = jnp.bfloat16


def dot(left, right):
    return jnp.dot(left, right, preferred_element_type=F32)


def dot_t(left, right):
    return lax.dot_general(left, right, (((1,), (1,)), ((), ())), preferred_element_type=F32)


def loop(low, high, body):
    def step(i, carry):
        body(i)
        return carry

    lax.fori_loop(low, high, step, 0)


def kernel(
    groups,
    columns,
    student,
    teacher,
    sims,
    projector,
    hard_group,
    hard_local,
    hard_count,
    text_weight,
    loss_out,
    student_out,
    projector_out,
    s_set,
    s_col,
    s_turned,
    proj,
    teach,
    sim_t,
    unit_t,
    cols_t,
    sim_s,
    exp_s,
    exp_t,
    row_total,
    h_mat,
    w_mat,
    back,
    comb,
    pair_rows,
    grad,
    grad_cols,
    facts,
    facts_set,
    facts_col,
    part,
    parts,
    hard_sum,
    totals,
    totals_set,
    within,
    arrived,
    loss_tile,
    loss_set,
    loss_tile2,
    loss_col,
    local_sem,
    set_send,
    set_recv,
    col_send,
    col_recv,
    unit_send,
    unit_recv,
    fset_send,
    fset_recv,
    fcol_send,
    fcol_recv,
    part_send,
    part_recv,
    tot_send,
    tot_recv,
    grad_send,
    grad_recv,
    out_send,
    out_recv,
    lset_send,
    lset_recv,
    lcol_send,
    lcol_recv,
):
    rows, width = student.shape
    chunk = unit_t.shape[2]
    count = unit_t.shape[0]
    half = rows // 2
    set_count = rows * columns
    g = lax.axis_index("group")
    d = lax.axis_index("dp")
    xs, zs = groups // 4, columns // 2
    x, yh, core = g // 4, lax.rem(g // 2, 2), lax.rem(g, 2)
    yl, z = d // zs, lax.rem(d, zs)

    def flip(value, by):
        return 1 - value if by else value

    def col_id(dx, fy, fc):
        return lax.rem(x + dx % xs, xs) * 4 + flip(yh, fy) * 2 + flip(core, fc)

    def set_id(fy, dz):
        return flip(yl, fy) * zs + lax.rem(z + dz % zs, zs)

    def rows_of(block):
        return pl.ds(pl.multiple_of(block * rows, rows), rows)

    def lanes_of(block):
        return pl.ds(pl.multiple_of(block * rows, rows), rows)

    def chunk_of(q):
        return pl.ds(pl.multiple_of(q * chunk, chunk), chunk)

    def copy(src, dst, send, recv, group, column):
        return pltpu.make_async_remote_copy(
            src_ref=src,
            dst_ref=dst,
            send_sem=send,
            recv_sem=recv,
            device_id=(group, column),
            device_id_type=MESH,
        )

    local = [
        pltpu.make_async_copy(student, s_set.at[rows_of(d)], local_sem.at[0]),
        pltpu.make_async_copy(student, s_col.at[rows_of(g)], local_sem.at[1]),
        pltpu.make_async_copy(teacher, teach, local_sem.at[2]),
        pltpu.make_async_copy(projector, proj, local_sem.at[3]),
        pltpu.make_async_copy(sims, sim_t, local_sem.at[4]),
    ]
    for one in (2, 0, 1, 3, 4):
        local[one].start()

    barrier = pltpu.get_barrier_semaphore()

    def greet(o):
        pl.semaphore_signal(
            barrier, inc=1, device_id=(g, lax.rem(d + o, columns)), device_id_type=MESH
        )
        pl.semaphore_signal(
            barrier, inc=1, device_id=(lax.rem(g + o, groups), d), device_id_type=MESH
        )

    loop(1, columns, greet)
    pl.semaphore_wait(barrier, 2 * (columns - 1))

    pending = []

    def region(ref, block, part_of):
        start = pl.multiple_of(block * rows, rows)
        if part_of is None:
            return ref.at[pl.ds(start, rows)]
        return ref.at[pl.ds(pl.multiple_of(start + part_of * half, half), half)]

    def set_slot(fy, dz, part_of):
        return (fy * zs + dz % zs) * 2 + (part_of or 0)

    def send_set(fy, dz, to_fy, to_dz, part_of=None):
        block = set_id(fy, dz)
        place = region(s_set, block, part_of)
        source = student if (fy == 0 and dz == 0) else place
        one = copy(
            source,
            place,
            set_send.at[len([p for p in pending if p[0] == "set"])],
            set_recv.at[set_slot(fy ^ to_fy, dz - to_dz, part_of)],
            g,
            set_id(to_fy, to_dz),
        )
        one.start()
        pending.append(("set", one))

    def wait_set(fy, dz, part_of=None):
        place = region(s_set, set_id(fy, dz), part_of)
        slot = set_slot(fy, dz, part_of)
        copy(place, place, set_send.at[0], set_recv.at[slot], g, set_id(1, 0)).wait_recv()

    def col_slot(dx, fy, fc, part_of):
        return ((fy * 2 + fc) * xs + dx % xs) * 2 + (part_of or 0)

    def send_col(dx, fy, to_dx, to_fy, to_fc, part_of=None):
        block = col_id(dx, fy, 0)
        place = region(s_col, block, part_of)
        source = student if (fy == 0 and dx == 0) else place
        one = copy(
            source,
            place,
            col_send.at[len([p for p in pending if p[0] == "col"])],
            col_recv.at[col_slot(dx - to_dx, fy ^ to_fy, to_fc, part_of)],
            col_id(to_dx, to_fy, to_fc),
            d,
        )
        one.start()
        pending.append(("col", one))

    def wait_col(dx, fy, fc, part_of=None):
        place = region(s_col, col_id(dx, fy, fc), part_of)
        slot = col_slot(dx, fy, fc, part_of)
        copy(place, place, col_send.at[0], col_recv.at[slot], col_id(0, 0, 1), d).wait_recv()

    send_set(0, 0, 1, 0)
    send_set(0, 0, 0, 1)
    send_set(0, 0, 0, -1)
    send_col(0, 0, 0, 1, 0)
    send_col(0, 0, 1, 0, 0)
    send_col(0, 0, -1, 0, 0)
    send_col(0, 0, 0, 0, 1)

    def pass_set(step):
        if step == 0:
            wait_set(1, 0)
            send_set(1, 0, 0, 1)
            send_set(1, 0, 0, -1)
            return
        last = step == zs // 2 - 1
        for fy in (0, 1):
            wait_set(fy, -step)
            send_set(fy, -step, 0, 1, 0 if last else None)
            wait_set(fy, step)
            send_set(fy, step, 0, -1, 1 if last else None)

    def pass_col(step):
        if step == 0:
            wait_col(0, 1, 0)
            send_col(0, 1, 1, 0, 0)
            send_col(0, 1, -1, 0, 0)
            send_col(0, 1, 0, 0, 1)
        elif step == 1:
            for fy in (0, 1):
                wait_col(-1, fy, 0)
                send_col(-1, fy, 1, 0, 0, 0)
                send_col(-1, fy, 0, 0, 1)
                wait_col(1, fy, 0)
                send_col(1, fy, -1, 0, 0, 1)
                send_col(1, fy, 0, 0, 1)
        else:
            for fy in (0, 1):
                wait_col(2, fy, 0, 0)
                wait_col(2, fy, 0, 1)
                send_col(2, fy, 0, 0, 1)

    def exchange(src_of, dst, send, recv, along):
        me, size = (d, columns) if along == "dp" else (g, groups)

        def at(o):
            peer = lax.rem(me + o, size)
            where = (g, peer) if along == "dp" else (peer, d)
            return copy(src_of(peer), dst(me), send.at[o], recv.at[o], *where)

        def arrive(o):
            source = lax.rem(me + size - o, size)
            where = (g, source) if along == "dp" else (source, d)
            copy(dst(source), dst(source), send.at[o], recv.at[o], *where).wait_recv()

        return (
            lambda: loop(1, size, lambda o: at(o).start()),
            lambda: loop(1, size, arrive),
            lambda: loop(1, size, lambda o: at(o).wait_send()),
        )

    local[2].wait()

    def square_sum(q, total):
        t = teach[:, chunk_of(q)].astype(F32)
        t = t * t
        return total + sum(t[:, i : i + 128] for i in range(0, chunk, 128))

    t_total = lax.fori_loop(0, count, square_sum, jnp.zeros((rows, 128), F32))
    t_scale = 1.0 / jnp.sqrt(jnp.sum(t_total, 1, keepdims=True) + EPSILON)

    def make_unit(q):
        unit_t[q] = (teach[:, chunk_of(q)].astype(F32) * t_scale).astype(BF16)

    loop(0, count, make_unit)
    unit_start, unit_wait, unit_end = exchange(
        lambda peer: unit_t.at[peer], lambda me: cols_t.at[rows_of(me)], unit_send, unit_recv, "group"
    )
    unit_start()
    cols_t[rows_of(g)] = unit_t[g]

    local[0].wait()
    local[1].wait()
    local[3].wait()
    back[...] = jnp.zeros_like(back)

    def project(q, carry):
        squares, along = carry
        p = dot(s_set[rows_of(d)], proj[:, chunk_of(q)])
        both = p * unit_t[q].astype(F32)
        back[...] += dot_t(p.astype(BF16), proj[:, chunk_of(q)])
        for i in range(0, chunk, 128):
            piece = p[:, i : i + 128]
            squares = squares + piece * piece
            along = along + both[:, i : i + 128]
        return squares, along

    zero = jnp.zeros((rows, 128), F32)
    squares, along = lax.fori_loop(0, count, project, (zero, zero))
    norm = jnp.sqrt(jnp.sum(squares, 1, keepdims=True) + EPSILON)
    cosine = jnp.sum(along, 1, keepdims=True)
    inverse = 1.0 / norm

    def split_store(value):
        high = value.astype(BF16)
        pair_rows[0:rows] = high
        pair_rows[rows : 2 * rows] = (value - high.astype(F32)).astype(BF16)

    split_store(back[...] * inverse)
    pass_set(0)
    pass_col(0)

    sub = lax.broadcasted_iota(jnp.int32, (rows, rows), 0)
    lane = lax.broadcasted_iota(jnp.int32, (rows, rows), 1)
    eye = sub == lane

    def to_row(column):
        return jnp.sum(jnp.where(eye, column, 0.0), 0, keepdims=True)

    def to_column(row):
        return jnp.sum(jnp.where(eye, row, 0.0), 1, keepdims=True)

    local[4].wait()

    def teacher_exp(b, total):
        value = jnp.exp(sim_t[:, lanes_of(b)] * INVERSE_TEMP)
        value = jnp.where(jnp.logical_and(eye, b == d), 0.0, value)
        exp_t[b] = value
        return total + value

    total_t = jnp.sum(lax.fori_loop(0, columns, teacher_exp, zero), 1, keepdims=True)
    weight_row = text_weight[...]
    used = hard_count[...]
    facts[0:1, :] = to_row(inverse)
    facts[1:2, :] = to_row(1.0 / total_t)
    facts[2:3, :] = weight_row
    for k in range(HARD):
        facts[3 + k : 4 + k, :] = (
            hard_group[k : k + 1, :] * rows + hard_local[k : k + 1, :]
        ).astype(F32)
        facts[5 + k : 6 + k, :] = (
            jnp.where(used > k, HARD_WEIGHT / used.astype(F32), 0.0) * weight_row
        )
    facts[7:8, :] = jnp.zeros((1, rows), F32)
    facts_set[d] = facts[...]
    facts_col[g] = facts[...]
    fcol_start, fcol_wait, fcol_end = exchange(
        lambda peer: facts, lambda me: facts_col.at[me], fcol_send, fcol_recv, "group"
    )
    fset_start, fset_wait, fset_end = exchange(
        lambda peer: facts, lambda me: facts_set.at[me], fset_send, fset_recv, "dp"
    )
    fcol_start()
    fset_start()
    pass_set(1)
    pass_col(1)

    row_total[...] = zero

    def similarity(block):
        both = dot_t(pair_rows[...], s_set[rows_of(block)])
        value = (both[0:rows] + both[rows : 2 * rows]) * facts_set[block, 0:1, :]
        grown = jnp.exp(value * INVERSE_TEMP)
        grown = jnp.where(jnp.logical_and(eye, block == d), 0.0, grown)
        sim_s[block] = value
        exp_s[block] = grown
        row_total[...] += grown

    def turn(block):
        s_turned[:, lanes_of(block)] = s_set[rows_of(block)].T

    unit_wait()
    fcol_wait()
    step_rows = 512 if groups * rows >= 512 else groups * rows
    numbers = lax.broadcasted_iota(jnp.int32, (step_rows, rows), 0).astype(F32)

    def pick(b):
        queries = cols_t[rows_of(b)]
        sums = [jnp.zeros((1, rows), F32)] * HARD
        for c in range(0, groups * rows, step_rows):
            gram = dot_t(cols_t[c : c + step_rows], queries)
            for k in range(HARD):
                wanted = facts_col[b, 3 + k : 4 + k, :] - float(c)
                sums[k] = sums[k] + jnp.sum(
                    jnp.where(numbers == wanted, gram, 0.0), 0, keepdims=True
                )
        for k in range(HARD):
            part[pl.ds(k * groups + b, 1), :] = sums[k]

    loop(0, groups, pick)
    part_start, part_wait, part_end = exchange(
        lambda peer: part, lambda me: parts.at[me], part_send, part_recv, "group"
    )
    part_start()
    parts[g] = part[...]
    pass_set(2)
    pass_col(2)

    fset_wait()
    for fy, dz in ((0, 0), (1, 0), (0, -1), (0, 1), (1, -1), (1, 1)):
        similarity(set_id(fy, dz))
    pass_set(3)
    for fy, dz in ((0, -2), (0, 2), (1, -2), (1, 2)):
        similarity(set_id(fy, dz))

    for dx in range(xs):
        for fy in (0, 1):
            wait_col(dx, fy, 1)
    part_wait()
    hard_sum[...] = jnp.sum(parts[...], 0)
    weight = to_column(weight_row)
    own_hard = [to_column(hard_sum[pl.ds(k * groups + g, 1), :]) for k in range(HARD)]
    own_target = [to_column(facts[3 + k : 4 + k, :]) for k in range(HARD)]
    own_entry = [to_column(facts[5 + k : 6 + k, :]) for k in range(HARD)]
    own_ids = sub.astype(F32) + (g * rows).astype(F32)
    lane_ids = lane.astype(F32)

    def hard(b, loss):
        both = dot_t(pair_rows[...], s_col[rows_of(b)])
        scale = facts_col[b, 0:1, :]
        cross = (both[0:rows] + both[rows : 2 * rows]) * scale
        ids = lane_ids + (b * rows).astype(F32)
        value = jnp.zeros_like(cross)
        for k in range(HARD):
            asked = jnp.where(ids == own_target[k], own_entry[k], 0.0)
            difference = cross - own_hard[k]
            term = asked * difference
            loss = loss + term * difference
            listed = jnp.where(
                facts_col[b, 3 + k : 4 + k, :] == own_ids, facts_col[b, 5 + k : 6 + k, :], 0.0
            )
            value = value + term + listed * (cross - hard_sum[pl.ds(k * groups + b, 1), :])
        h_mat[:, lanes_of(b)] = (2.0 * scale * value).astype(BF16)
        return loss

    hard_loss = lax.fori_loop(0, groups, hard, zero)
    for fy, dz in ((0, -3), (0, 3), (1, -3), (1, 3)):
        similarity(set_id(fy, dz))
    for fy in (0, 1):
        wait_set(fy, zs // 2, 0)
        wait_set(fy, zs // 2, 1)
        similarity(set_id(fy, zs // 2))

    total_s = jnp.sum(row_total[...], 1, keepdims=True)
    totals[...] = jnp.broadcast_to(to_row(1.0 / total_s), totals.shape)
    totals_set[d] = totals[...]
    tot_start, tot_wait, tot_end = exchange(
        lambda peer: totals, lambda me: totals_set.at[me], tot_send, tot_recv, "dp"
    )
    tot_start()
    piece = 256 if width >= 256 else width
    for n in range(0, width, piece):
        comb[:, n : n + piece] = dot(h_mat[...], s_col[:, n : n + piece])
    loop(0, columns, turn)
    tot_wait()

    scale_s, scale_t = weight / total_s, weight / total_t

    def pairs(b, carry):
        squares, divergence = carry
        value = sim_s[b]
        gap = value - sim_t[:, lanes_of(b)]
        their = facts_set[b, 2:3, :]
        student_part = exp_s[b] * (scale_s + their * totals_set[b, 0:1, :])
        teacher_part = exp_t[b] * (scale_t + their * facts_set[b, 1:2, :])
        pair = (2.0 * SIMILARITY_COEF / set_count) * gap * (weight + their) + INVERSE_TEMP * (
            student_part - teacher_part
        )
        w_mat[:, lanes_of(b)] = (pair * facts_set[b, 0:1, :]).astype(BF16)
        return squares + gap * gap, divergence + exp_t[b] * gap

    squares, divergence = lax.fori_loop(0, columns, pairs, (zero, zero))
    for n in range(0, width, piece):
        comb[:, n : n + piece] += dot(w_mat[...], s_set[:, n : n + piece])
    combined = comb[...] * LOSS_SCALE
    inner = jnp.sum(back[...] * combined, 1, keepdims=True) - LOSS_SCALE * weight * cosine
    split_store(
        combined * inverse
        - s_set[rows_of(d)].astype(F32) * (inner * inverse * inverse * inverse)
    )
    teacher_scale = LOSS_SCALE * weight * inverse

    def gradient(q):
        both = dot(pair_rows[...], proj[:, chunk_of(q)])
        value = both[0:rows] + both[rows : 2 * rows] - teacher_scale * unit_t[q].astype(F32)
        grad[q] = value.astype(BF16)

    def grad_copy(o):
        peer = lax.rem(d + o, columns)
        return copy(
            grad.at[peer], grad_cols.at[rows_of(d)], grad_send.at[o], grad_recv.at[o], g, peer
        )

    def gradient_step(o):
        gradient(lax.rem(d + o, columns))
        grad_copy(o).start()

    loop(1, columns, gradient_step)
    gradient(d)
    grad_cols[rows_of(d)] = grad[d]

    sim_term = (SIMILARITY_COEF / set_count) * jnp.sum(squares, 1, keepdims=True)
    kl_term = (
        jnp.log(total_s)
        - jnp.log(total_t)
        - INVERSE_TEMP * jnp.sum(divergence, 1, keepdims=True) / total_t
    )
    per_text = weight * (1.0 - cosine * inverse + sim_term + kl_term) + jnp.sum(
        hard_loss, 1, keepdims=True
    )
    loss_tile[...] = jnp.broadcast_to(jnp.sum(per_text, 0, keepdims=True), loss_tile.shape)
    loss_set[d] = loss_tile[...]
    lset_start, lset_wait, lset_end = exchange(
        lambda peer: loss_tile, lambda me: loss_set.at[me], lset_send, lset_recv, "dp"
    )
    lset_start()

    comb[...] = jnp.zeros_like(comb)

    def student_part(q):
        comb[...] += dot_t(grad[q], proj[:, chunk_of(q)])

    loop(0, count, student_part)
    student_out[...] = comb[...].astype(BF16)

    lset_wait()
    loss_tile2[...] = jnp.sum(loss_set[...], 0)
    loss_col[g] = loss_tile2[...]
    lcol_start, lcol_wait, lcol_end = exchange(
        lambda peer: loss_tile2, lambda me: loss_col.at[me], lcol_send, lcol_recv, "group"
    )
    lcol_start()

    def grad_arrive(o):
        source = lax.rem(d + columns - o, columns)
        place = grad_cols.at[rows_of(source)]
        copy(place, place, grad_send.at[o], grad_recv.at[o], g, source).wait_recv()

    loop(1, columns, grad_arrive)
    share = width // groups
    for n in range(0, width, piece):
        result = dot(s_turned[n : n + piece, :], grad_cols[...]).astype(BF16)
        for i in range(piece // share):
            within[n // share + i] = result[i * share : (i + 1) * share]
    out_start, out_wait, out_end = exchange(
        lambda peer: within.at[peer], lambda me: arrived.at[me], out_send, out_recv, "group"
    )
    out_start()
    arrived[g] = within[g]
    lcol_wait()
    loss_out[0, 0] = jnp.sum(loss_col[...]) * (
        1.0 / (8.0 * 128.0 * rows * groups * columns)
    )
    out_wait()
    projector_out[...] = jnp.sum(arrived[...].astype(F32), 0)

    for _, one in pending:
        one.wait_send()
    loop(1, columns, lambda o: grad_copy(o).wait_send())
    for end in (unit_end, fcol_end, fset_end, part_end, tot_end, lset_end, lcol_end, out_end):
        end()


def local_program(
    student, teacher, teacher_similarity, projector, hard_group, hard_local, hard_count, text_weight
):
    rows, width = student.shape
    groups = lax.axis_size("group")
    columns = lax.axis_size("dp")
    wide = projector.shape[1]
    chunk = wide // groups
    dma = pltpu.SemaphoreType.DMA
    vm = pltpu.VMEM
    texts, col_texts = rows * columns, rows * groups
    scratch = [
        vm((texts, width), BF16),
        vm((col_texts, width), BF16),
        vm((width, texts), BF16),
        vm((width, wide), BF16),
        vm((rows, wide), BF16),
        vm((rows, texts), F32),
        vm((groups, rows, chunk), BF16),
        vm((col_texts, chunk), BF16),
        vm((columns, rows, rows), F32),
        vm((columns, rows, rows), F32),
        vm((columns, rows, rows), F32),
        vm((rows, rows), F32),
        vm((rows, col_texts), BF16),
        vm((rows, texts), BF16),
        vm((rows, width), F32),
        vm((rows, width), F32),
        vm((2 * rows, width), BF16),
        vm((groups, rows, chunk), BF16),
        vm((texts, chunk), BF16),
        vm((8, rows), F32),
        vm((columns, 8, rows), F32),
        vm((groups, 8, rows), F32),
        vm((HARD * groups, rows), F32),
        vm((groups, HARD * groups, rows), F32),
        vm((HARD * groups, rows), F32),
        vm((8, rows), F32),
        vm((columns, 8, rows), F32),
        vm((groups, width // groups, chunk), BF16),
        vm((groups, width // groups, chunk), BF16),
        vm((8, 128), F32),
        vm((columns, 8, 128), F32),
        vm((8, 128), F32),
        vm((groups, 8, 128), F32),
        dma((5,)),
        dma((2 * columns + 2,)),
        dma((2 * columns,)),
        dma((2 * groups,)),
        dma((2 * groups,)),
    ] + [dma((groups,)) for _ in range(18)]
    anywhere = pl.BlockSpec(memory_space=pl.ANY)
    vmem = pl.BlockSpec(memory_space=pltpu.VMEM)
    loss, student_gradient, projector_gradient = pl.pallas_call(
        functools.partial(kernel, groups, columns),
        out_shape=(
            jax.ShapeDtypeStruct((1, 1), F32),
            jax.ShapeDtypeStruct((rows, width), BF16),
            jax.ShapeDtypeStruct((width // groups, wide // columns), F32),
        ),
        in_specs=[anywhere] * 4 + [vmem] * 4,
        out_specs=(pl.BlockSpec(memory_space=pltpu.SMEM), vmem, vmem),
        scratch_shapes=scratch,
        compiler_params=pltpu.CompilerParams(
            collective_id=0, has_side_effects=True, vmem_limit_bytes=58 * 1024 * 1024
        ),
        cost_estimate=pl.CostEstimate(
            flops=12_000_000_000, bytes_accessed=16_000_000, transcendentals=1_000_000
        ),
    )(
        student,
        teacher,
        teacher_similarity,
        projector,
        hard_group.T,
        hard_local.T,
        hard_count.reshape(1, rows),
        text_weight.reshape(1, rows),
    )
    return loss.reshape(()), student_gradient, projector_gradient


def solution(mesh):
    return jax.shard_map(
        local_program,
        mesh=mesh,
        in_specs=(
            P(("group", "dp"), None),
            P(("group", "dp"), None),
            P(("group", "dp"), None),
            P(),
            P(("group", "dp"), None),
            P(("group", "dp"), None),
            P(("group", "dp")),
            P(("group", "dp")),
        ),
        out_specs=(P(), P(("group", "dp"), None), P("group", "dp")),
        check_vma=False,
    )
```

```python
import functools
import jax
import jax.numpy as jnp
from jax import lax
from jax.experimental import pallas as pl
from jax.experimental.pallas import tpu as pltpu
from jax.sharding import PartitionSpec as P

HARD = 2
EPSILON = 1e-06
INVERSE_TEMP = 20.0
SIMILARITY_COEF = 200.0
HARD_WEIGHT = 20.0
LOSS_SCALE = 1024.0
MESH = pl.DeviceIdType.MESH
F32 = jnp.float32
BF16 = jnp.bfloat16


def dot(left, right):
    return jnp.dot(left, right, preferred_element_type=F32)


def dot_t(left, right):
    return lax.dot_general(left, right, (((1,), (1,)), ((), ())), preferred_element_type=F32)


def loop(low, high, body):
    def step(i, carry):
        body(i)
        return carry

    lax.fori_loop(low, high, step, 0)


def kernel(
    groups,
    columns,
    student,
    teacher,
    sims,
    projector,
    hard_group,
    hard_local,
    hard_count,
    text_weight,
    loss_out,
    student_out,
    projector_out,
    s_set,
    s_col,
    s_turned,
    c_turned,
    proj,
    teach,
    sim_t,
    unit_t,
    cols_t,
    sim_s,
    exp_s,
    exp_t,
    cross_s,
    row_total,
    h_mat,
    w_mat,
    back,
    comb,
    pair_rows,
    grad,
    grad_cols,
    facts,
    facts_set,
    facts_col,
    part,
    parts,
    hard_sum,
    totals,
    totals_set,
    within,
    arrived,
    mirror_out,
    mirror_in,
    loss_tile,
    loss_set,
    loss_tile2,
    loss_col,
    local_sem,
    set_send,
    set_recv,
    col_send,
    col_recv,
    unit_send,
    unit_recv,
    fset_send,
    fset_recv,
    fcol_send,
    fcol_recv,
    part_send,
    part_recv,
    tot_send,
    tot_recv,
    grad_send,
    grad_recv,
    out_send,
    out_recv,
    lset_send,
    lset_recv,
    lcol_send,
    lcol_recv,
    mirror_sem,
):
    rows, width = student.shape
    chunk = unit_t.shape[2]
    count = unit_t.shape[0]
    half = rows // 2
    set_count = rows * columns
    g = lax.axis_index("group")
    d = lax.axis_index("dp")
    xs, zs = groups // 4, columns // 2
    x, yh, core = g // 4, lax.rem(g // 2, 2), lax.rem(g, 2)
    yl, z = d // zs, lax.rem(d, zs)

    def flip(value, by):
        return 1 - value if by else value

    def col_id(dx, fy, fc):
        return lax.rem(x + dx % xs, xs) * 4 + flip(yh, fy) * 2 + flip(core, fc)

    def set_id(fy, dz):
        return flip(yl, fy) * zs + lax.rem(z + dz % zs, zs)

    def rows_of(block):
        return pl.ds(pl.multiple_of(block * rows, rows), rows)

    def lanes_of(block):
        return pl.ds(pl.multiple_of(block * rows, rows), rows)

    def chunk_of(q):
        return pl.ds(pl.multiple_of(q * chunk, chunk), chunk)

    def copy(src, dst, send, recv, group, column):
        return pltpu.make_async_remote_copy(
            src_ref=src,
            dst_ref=dst,
            send_sem=send,
            recv_sem=recv,
            device_id=(group, column),
            device_id_type=MESH,
        )

    local = [
        pltpu.make_async_copy(student, s_set.at[rows_of(d)], local_sem.at[0]),
        pltpu.make_async_copy(student, s_col.at[rows_of(g)], local_sem.at[1]),
        pltpu.make_async_copy(teacher, teach, local_sem.at[2]),
        pltpu.make_async_copy(projector, proj, local_sem.at[3]),
        pltpu.make_async_copy(sims, sim_t, local_sem.at[4]),
    ]
    for one in (2, 0, 1, 3, 4):
        local[one].start()

    barrier = pltpu.get_barrier_semaphore()

    def greet(o):
        pl.semaphore_signal(
            barrier, inc=1, device_id=(g, lax.rem(d + o, columns)), device_id_type=MESH
        )
        pl.semaphore_signal(
            barrier, inc=1, device_id=(lax.rem(g + o, groups), d), device_id_type=MESH
        )

    loop(1, columns, greet)

    @pl.when(g != d)
    def greet_mirror():
        pl.semaphore_signal(barrier, inc=1, device_id=(d, g), device_id_type=MESH)

    local[2].wait()

    def square_sum(q, total):
        t = teach[:, chunk_of(q)].astype(F32)
        t = t * t
        return total + sum(t[:, i : i + 128] for i in range(0, chunk, 128))

    t_total = lax.fori_loop(0, count, square_sum, jnp.zeros((rows, 128), F32))
    t_scale = 1.0 / jnp.sqrt(jnp.sum(t_total, 1, keepdims=True) + EPSILON)

    def make_unit(q):
        unit_t[q] = (teach[:, chunk_of(q)].astype(F32) * t_scale).astype(BF16)

    loop(0, count, make_unit)
    others = (lax.rem(g - d + groups, groups) + groups - 1) // groups
    pl.semaphore_wait(barrier, 2 * (columns - 1) + others)

    pending = []

    def region(ref, block, part_of):
        start = pl.multiple_of(block * rows, rows)
        if part_of is None:
            return ref.at[pl.ds(start, rows)]
        return ref.at[pl.ds(pl.multiple_of(start + part_of * half, half), half)]

    def set_slot(fy, dz, part_of):
        return (fy * zs + dz % zs) * 2 + (part_of or 0)

    def send_set(fy, dz, to_fy, to_dz, part_of=None):
        block = set_id(fy, dz)
        place = region(s_set, block, part_of)
        source = student if (fy == 0 and dz == 0) else place
        one = copy(
            source,
            place,
            set_send.at[len([p for p in pending if p[0] == "set"])],
            set_recv.at[set_slot(fy ^ to_fy, dz - to_dz, part_of)],
            g,
            set_id(to_fy, to_dz),
        )
        one.start()
        pending.append(("set", one))

    def wait_set(fy, dz, part_of=None):
        place = region(s_set, set_id(fy, dz), part_of)
        slot = set_slot(fy, dz, part_of)
        copy(place, place, set_send.at[0], set_recv.at[slot], g, set_id(1, 0)).wait_recv()

    def col_slot(dx, fy, fc, part_of):
        return ((fy * 2 + fc) * xs + dx % xs) * 2 + (part_of or 0)

    def send_col(dx, fy, to_dx, to_fy, to_fc, part_of=None):
        block = col_id(dx, fy, 0)
        place = region(s_col, block, part_of)
        source = student if (fy == 0 and dx == 0) else place
        one = copy(
            source,
            place,
            col_send.at[len([p for p in pending if p[0] == "col"])],
            col_recv.at[col_slot(dx - to_dx, fy ^ to_fy, to_fc, part_of)],
            col_id(to_dx, to_fy, to_fc),
            d,
        )
        one.start()
        pending.append(("col", one))

    def wait_col(dx, fy, fc, part_of=None):
        place = region(s_col, col_id(dx, fy, fc), part_of)
        slot = col_slot(dx, fy, fc, part_of)
        copy(place, place, col_send.at[0], col_recv.at[slot], col_id(0, 0, 1), d).wait_recv()

    send_set(0, 0, 1, 0)
    send_set(0, 0, 0, 1)
    send_set(0, 0, 0, -1)
    send_col(0, 0, 0, 1, 0)
    send_col(0, 0, 1, 0, 0)
    send_col(0, 0, -1, 0, 0)
    send_col(0, 0, 0, 0, 1)

    def pass_set(step):
        if step == 0:
            wait_set(1, 0)
            send_set(1, 0, 0, 1)
            send_set(1, 0, 0, -1)
            return
        last = step == zs // 2 - 1
        for fy in (0, 1):
            wait_set(fy, -step)
            send_set(fy, -step, 0, 1, 0 if last else None)
            wait_set(fy, step)
            send_set(fy, step, 0, -1, 1 if last else None)

    def pass_col(step):
        if step == 0:
            wait_col(0, 1, 0)
            send_col(0, 1, 1, 0, 0)
            send_col(0, 1, -1, 0, 0)
            send_col(0, 1, 0, 0, 1)
        elif step == 1:
            for fy in (0, 1):
                wait_col(-1, fy, 0)
                send_col(-1, fy, 1, 0, 0, 0)
                send_col(-1, fy, 0, 0, 1)
                wait_col(1, fy, 0)
                send_col(1, fy, -1, 0, 0, 1)
                send_col(1, fy, 0, 0, 1)
        else:
            for fy in (0, 1):
                wait_col(2, fy, 0, 0)
                wait_col(2, fy, 0, 1)
                send_col(2, fy, 0, 0, 1)

    def exchange(src_of, dst, send, recv, along):
        me, size = (d, columns) if along == "dp" else (g, groups)

        def at(o):
            peer = lax.rem(me + o, size)
            where = (g, peer) if along == "dp" else (peer, d)
            return copy(src_of(peer), dst(me), send.at[o], recv.at[o], *where)

        def arrive(o):
            source = lax.rem(me + size - o, size)
            where = (g, source) if along == "dp" else (source, d)
            copy(dst(source), dst(source), send.at[o], recv.at[o], *where).wait_recv()

        return (
            lambda: loop(1, size, lambda o: at(o).start()),
            lambda: loop(1, size, arrive),
            lambda: loop(1, size, lambda o: at(o).wait_send()),
        )

    unit_start, unit_wait, unit_end = exchange(
        lambda peer: unit_t.at[peer], lambda me: cols_t.at[rows_of(me)], unit_send, unit_recv, "group"
    )
    unit_start()
    cols_t[rows_of(g)] = unit_t[g]

    local[0].wait()
    local[1].wait()
    local[3].wait()
    back[...] = jnp.zeros_like(back)

    def project(q, carry):
        squares, along = carry
        p = dot(s_set[rows_of(d)], proj[:, chunk_of(q)])
        both = p * unit_t[q].astype(F32)
        back[...] += dot_t(p.astype(BF16), proj[:, chunk_of(q)])
        for i in range(0, chunk, 128):
            piece = p[:, i : i + 128]
            squares = squares + piece * piece
            along = along + both[:, i : i + 128]
        return squares, along

    zero = jnp.zeros((rows, 128), F32)
    squares, along = lax.fori_loop(0, count, project, (zero, zero))
    norm = jnp.sqrt(jnp.sum(squares, 1, keepdims=True) + EPSILON)
    cosine = jnp.sum(along, 1, keepdims=True)
    inverse = 1.0 / norm

    def split_store(value):
        high = value.astype(BF16)
        pair_rows[0:rows] = high
        pair_rows[rows : 2 * rows] = (value - high.astype(F32)).astype(BF16)

    split_store(back[...] * inverse)
    pass_set(0)

    sub = lax.broadcasted_iota(jnp.int32, (rows, rows), 0)
    lane = lax.broadcasted_iota(jnp.int32, (rows, rows), 1)
    eye = sub == lane

    def to_row(column):
        return jnp.sum(jnp.where(eye, column, 0.0), 0, keepdims=True)

    def to_column(row):
        return jnp.sum(jnp.where(eye, row, 0.0), 1, keepdims=True)

    local[4].wait()

    def teacher_exp(b, total):
        value = jnp.exp(sim_t[:, lanes_of(b)] * INVERSE_TEMP)
        value = jnp.where(jnp.logical_and(eye, b == d), 0.0, value)
        exp_t[b] = value
        return total + value

    total_t = jnp.sum(lax.fori_loop(0, columns, teacher_exp, zero), 1, keepdims=True)
    weight_row = text_weight[...]
    used = hard_count[...]
    facts[0:1, :] = to_row(inverse)
    facts[1:2, :] = to_row(1.0 / total_t)
    facts[2:3, :] = weight_row
    for k in range(HARD):
        facts[3 + k : 4 + k, :] = (
            hard_group[k : k + 1, :] * rows + hard_local[k : k + 1, :]
        ).astype(F32)
        facts[5 + k : 6 + k, :] = (
            jnp.where(used > k, HARD_WEIGHT / used.astype(F32), 0.0) * weight_row
        )
    facts[7:8, :] = jnp.zeros((1, rows), F32)
    facts_set[d] = facts[...]
    facts_col[g] = facts[...]
    fcol_start, fcol_wait, fcol_end = exchange(
        lambda peer: facts, lambda me: facts_col.at[me], fcol_send, fcol_recv, "group"
    )
    fset_start, fset_wait, fset_end = exchange(
        lambda peer: facts, lambda me: facts_set.at[me], fset_send, fset_recv, "dp"
    )
    fcol_start()
    fset_start()
    pass_set(1)
    pass_col(0)

    row_total[...] = zero

    def multiply(block):
        both = dot_t(pair_rows[...], s_set[rows_of(block)])
        sim_s[block] = both[0:rows] + both[rows : 2 * rows]
        s_turned[:, lanes_of(block)] = s_set[rows_of(block)].T

    def finish(block):
        value = sim_s[block] * facts_set[block, 0:1, :]
        grown = jnp.exp(value * INVERSE_TEMP)
        grown = jnp.where(jnp.logical_and(eye, block == d), 0.0, grown)
        sim_s[block] = value
        exp_s[block] = grown
        row_total[...] += grown

    for fy, dz in ((0, 0), (1, 0), (0, -1), (0, 1), (1, -1), (1, 1)):
        multiply(set_id(fy, dz))
    pass_set(2)
    pass_col(1)
    for fy, dz in ((0, -2), (0, 2), (1, -2), (1, 2)):
        multiply(set_id(fy, dz))

    unit_wait()
    fcol_wait()
    numbers = lax.broadcasted_iota(jnp.int32, (rows, 2 * rows), 0).astype(F32)
    step_blocks = 4

    def pick(b):
        queries = cols_t[pl.ds(pl.multiple_of(2 * b * rows, 2 * rows), 2 * rows)]
        first, second = [
            jnp.concatenate([facts_col[2 * b + i, 3 + k : 4 + k, :] for i in (0, 1)], 1)
            for k in range(HARD)
        ]
        sums = [jnp.zeros((1, 2 * rows), F32)] * HARD
        for c in range(0, groups, step_blocks):
            gram = dot_t(cols_t[c * rows : (c + step_blocks) * rows], queries)
            for j in range(step_blocks):
                low = float((c + j) * rows)
                here = jnp.logical_and(first >= low, first < low + rows)
                wanted = jnp.where(here, first, second) - low
                found = jnp.sum(
                    jnp.where(numbers == wanted, gram[j * rows : (j + 1) * rows], 0.0),
                    0,
                    keepdims=True,
                )
                sums[0] = sums[0] + jnp.where(here, found, 0.0)
                sums[1] = sums[1] + jnp.where(here, 0.0, found)
        for k in range(HARD):
            for i in (0, 1):
                part[pl.ds(k * groups + 2 * b + i, 1), :] = sums[k][:, i * rows : (i + 1) * rows]

    loop(0, groups // 4, pick)
    pass_set(3)
    pass_col(2)
    loop(groups // 4, groups // 2, pick)
    part_start, part_wait, part_end = exchange(
        lambda peer: part, lambda me: parts.at[me], part_send, part_recv, "group"
    )
    part_start()
    parts[g] = part[...]
    for fy, dz in ((0, -3), (0, 3), (1, -3), (1, 3)):
        multiply(set_id(fy, dz))
    fset_wait()

    def finish_near(i):
        fy, dz = i // (zs - 1), lax.rem(i, zs - 1) - (zs // 2 - 1)
        finish((yl + fy - 2 * fy * yl) * zs + lax.rem(z + dz + zs, zs))

    loop(0, 2 * (zs - 1), finish_near)
    for dx in range(xs):
        for fy in (0, 1):
            wait_col(dx, fy, 1)

    def cross_pair(b):
        both = dot_t(
            pair_rows[...], s_col[pl.ds(pl.multiple_of(2 * b * rows, 2 * rows), 2 * rows)]
        )
        value = both[0:rows] + both[rows : 2 * rows]
        for i in (0, 1):
            cross_s[2 * b + i] = (
                value[:, i * rows : (i + 1) * rows] * facts_col[2 * b + i, 0:1, :]
            )

    loop(0, groups // 2, cross_pair)
    for fy in (0, 1):
        wait_set(fy, zs // 2, 0)
        wait_set(fy, zs // 2, 1)
        far = set_id(fy, zs // 2)
        multiply(far)
        finish(far)
    total_s = jnp.sum(row_total[...], 1, keepdims=True)
    totals[...] = jnp.broadcast_to(to_row(1.0 / total_s), totals.shape)
    totals_set[d] = totals[...]
    tot_start, tot_wait, tot_end = exchange(
        lambda peer: totals, lambda me: totals_set.at[me], tot_send, tot_recv, "dp"
    )
    tot_start()

    part_wait()
    hard_sum[...] = jnp.sum(parts[...], 0)
    weight = to_column(weight_row)
    own_hard = [to_column(hard_sum[pl.ds(k * groups + g, 1), :]) for k in range(HARD)]
    own_target = [to_column(facts[3 + k : 4 + k, :]) for k in range(HARD)]
    own_entry = [to_column(facts[5 + k : 6 + k, :]) for k in range(HARD)]
    own_ids = sub.astype(F32) + (g * rows).astype(F32)
    lane_ids = lane.astype(F32)

    def hard(b, loss):
        scale = facts_col[b, 0:1, :]
        cross = cross_s[b]
        ids = lane_ids + (b * rows).astype(F32)
        value = jnp.zeros_like(cross)
        for k in range(HARD):
            asked = jnp.where(ids == own_target[k], own_entry[k], 0.0)
            difference = cross - own_hard[k]
            term = asked * difference
            loss = loss + term * difference
            listed = jnp.where(
                facts_col[b, 3 + k : 4 + k, :] == own_ids, facts_col[b, 5 + k : 6 + k, :], 0.0
            )
            value = value + term + listed * (cross - hard_sum[pl.ds(k * groups + b, 1), :])
        h_mat[:, lanes_of(b)] = (2.0 * scale * value).astype(BF16)
        return loss

    hard_loss = lax.fori_loop(0, groups, hard, zero)
    piece = 256 if width >= 256 else width
    for n in range(0, width, piece):
        comb[:, n : n + piece] = dot(h_mat[...], s_col[:, n : n + piece])
    scale_s, scale_t = weight / total_s, weight / total_t

    def pairs(b, carry):
        squares, divergence = carry
        gap = sim_s[b] - sim_t[:, lanes_of(b)]
        their = facts_set[b, 2:3, :]
        grown = exp_t[b]
        sim_s[b] = (2.0 * SIMILARITY_COEF / set_count) * gap * (
            weight + their
        ) + INVERSE_TEMP * (exp_s[b] * scale_s - grown * (scale_t + their * facts_set[b, 1:2, :]))
        return squares + gap * gap, divergence + grown * gap

    squares, divergence = lax.fori_loop(0, columns, pairs, (zero, zero))
    tot_wait()

    def complete(b):
        their = INVERSE_TEMP * facts_set[b, 2:3, :] * totals_set[b, 0:1, :]
        w_mat[:, lanes_of(b)] = (
            (sim_s[b] + exp_s[b] * their) * facts_set[b, 0:1, :]
        ).astype(BF16)

    loop(0, columns, complete)
    for n in range(0, width, piece):
        comb[:, n : n + piece] += dot(w_mat[...], s_set[:, n : n + piece])
    combined = comb[...] * LOSS_SCALE
    inner = jnp.sum(back[...] * combined, 1, keepdims=True) - LOSS_SCALE * weight * cosine
    split_store(
        combined * inverse
        - s_set[rows_of(d)].astype(F32) * (inner * inverse * inverse * inverse)
    )
    thin = chunk // 2
    teacher_scale = LOSS_SCALE * weight * inverse

    def gradient(q):
        both = dot(pair_rows[...], proj[:, chunk_of(q)])
        value = both[0:rows] + both[rows : 2 * rows] - teacher_scale * unit_t[q].astype(F32)
        for h in (0, 1):
            grad[h, q] = value[:, h * thin : (h + 1) * thin].astype(BF16)

    def set_copy(o):
        peer = lax.rem(d + o, columns)
        return copy(
            grad.at[0, peer],
            grad_cols.at[0, rows_of(d)],
            grad_send.at[0, o],
            grad_recv.at[0, o],
            g,
            peer,
        )

    def col_copy(o):
        peer = lax.rem(g + o, groups)
        return copy(
            grad.at[1, peer],
            grad_cols.at[1, rows_of(g)],
            grad_send.at[1, o],
            grad_recv.at[1, o],
            peer,
            d,
        )

    def gradient_step(o):
        q = lax.rem(d + o, columns)
        gradient(q)
        apart = lax.rem(q + groups - g, groups)

        @pl.when(apart != 0)
        def send_col_part():
            col_copy(apart).start()

        @pl.when(o != columns)
        def send_set_part():
            set_copy(o).start()

    loop(1, columns + 1, gradient_step)
    grad_cols[0, rows_of(d)] = grad[0, d]
    grad_cols[1, rows_of(g)] = grad[1, g]

    sim_term = (SIMILARITY_COEF / set_count) * jnp.sum(squares, 1, keepdims=True)
    kl_term = (
        jnp.log(total_s)
        - jnp.log(total_t)
        - INVERSE_TEMP * jnp.sum(divergence, 1, keepdims=True) / total_t
    )
    per_text = weight * (1.0 - cosine * inverse + sim_term + kl_term) + jnp.sum(
        hard_loss, 1, keepdims=True
    )
    loss_tile[...] = jnp.broadcast_to(jnp.sum(per_text, 0, keepdims=True), loss_tile.shape)
    loss_set[d] = loss_tile[...]
    lset_start, lset_wait, lset_end = exchange(
        lambda peer: loss_tile, lambda me: loss_set.at[me], lset_send, lset_recv, "dp"
    )
    lset_start()

    def turn_col(b):
        c_turned[:, lanes_of(b)] = s_col[rows_of(b)].T

    loop(0, groups, turn_col)

    def set_arrive(o):
        source = lax.rem(d + columns - o, columns)
        place = grad_cols.at[0, rows_of(source)]
        copy(place, place, grad_send.at[0, o], grad_recv.at[0, o], g, source).wait_recv()

    def col_arrive(o):
        source = lax.rem(g + groups - o, groups)
        place = grad_cols.at[1, rows_of(source)]
        copy(place, place, grad_send.at[1, o], grad_recv.at[1, o], source, d).wait_recv()

    share = width // groups

    def products(h, turned):
        for n in range(0, width, piece):
            result = dot(turned[n : n + piece, :], grad_cols[h]).astype(BF16)
            for i in range(piece // share):
                within[h, n // share + i] = result[i * share : (i + 1) * share]

    def out_exchange(h, along):
        return exchange(
            lambda peer: within.at[h, peer],
            lambda me: arrived.at[h, me],
            out_send.at[h],
            out_recv.at[h],
            along,
        )

    loop(1, groups, col_arrive)
    products(1, c_turned)
    out1_start, out1_wait, out1_end = out_exchange(1, "dp")
    out1_start()
    arrived[1, d] = within[1, d]

    comb[...] = jnp.zeros_like(comb)

    def student_part(q):
        both = jnp.concatenate([grad[0, q], grad[1, q]], 1)
        comb[...] += dot_t(both, proj[:, chunk_of(q)])

    loop(0, count, student_part)
    student_out[...] = comb[...].astype(BF16)

    for _, one in pending:
        one.wait_send()
    for end in (unit_end, fcol_end, fset_end, part_end, tot_end):
        end()
    lset_wait()
    loss_tile2[...] = jnp.sum(loss_set[...], 0)
    loss_col[g] = loss_tile2[...]
    lcol_start, lcol_wait, lcol_end = exchange(
        lambda peer: loss_tile2, lambda me: loss_col.at[me], lcol_send, lcol_recv, "group"
    )
    lcol_start()

    loop(1, columns, set_arrive)
    products(0, s_turned)
    out0_start, out0_wait, out0_end = out_exchange(0, "group")
    out0_start()
    arrived[0, g] = within[0, g]
    out1_wait()
    mirror_out[...] = jnp.sum(arrived[1].astype(F32), 0)
    mirror = copy(mirror_out, mirror_in, mirror_sem.at[0], mirror_sem.at[1], d, g)

    @pl.when(g != d)
    def send_mirror():
        mirror.start()

    lcol_wait()
    loss_out[0, 0] = jnp.sum(loss_col[...]) * (
        1.0 / (8.0 * 128.0 * rows * groups * columns)
    )
    out0_wait()
    projector_out[:, :thin] = jnp.sum(arrived[0].astype(F32), 0)

    @pl.when(g != d)
    def take_mirror():
        mirror.wait()
        projector_out[:, thin:] = mirror_in[...]

    @pl.when(g == d)
    def keep_own():
        projector_out[:, thin:] = mirror_out[...]

    loop(1, columns, lambda o: set_copy(o).wait_send())
    loop(1, groups, lambda o: col_copy(o).wait_send())
    for end in (lset_end, lcol_end, out0_end, out1_end):
        end()


def local_program(
    student, teacher, teacher_similarity, projector, hard_group, hard_local, hard_count, text_weight
):
    rows, width = student.shape
    groups = lax.axis_size("group")
    columns = lax.axis_size("dp")
    wide = projector.shape[1]
    chunk = wide // groups
    dma = pltpu.SemaphoreType.DMA
    vm = pltpu.VMEM
    texts, col_texts = rows * columns, rows * groups
    scratch = [
        vm((texts, width), BF16),
        vm((col_texts, width), BF16),
        vm((width, texts), BF16),
        vm((width, col_texts), BF16),
        vm((width, wide), BF16),
        vm((rows, wide), BF16),
        vm((rows, texts), F32),
        vm((groups, rows, chunk), BF16),
        vm((col_texts, chunk), BF16),
        vm((columns, rows, rows), F32),
        vm((columns, rows, rows), F32),
        vm((columns, rows, rows), F32),
        vm((groups, rows, rows), F32),
        vm((rows, rows), F32),
        vm((rows, col_texts), BF16),
        vm((rows, texts), BF16),
        vm((rows, width), F32),
        vm((rows, width), F32),
        vm((2 * rows, width), BF16),
        vm((2, columns, rows, chunk // 2), BF16),
        vm((2, texts, chunk // 2), BF16),
        vm((8, rows), F32),
        vm((columns, 8, rows), F32),
        vm((groups, 8, rows), F32),
        vm((HARD * groups, rows), F32),
        vm((groups, HARD * groups, rows), F32),
        vm((HARD * groups, rows), F32),
        vm((8, rows), F32),
        vm((columns, 8, rows), F32),
        vm((2, groups, width // groups, chunk // 2), BF16),
        vm((2, groups, width // groups, chunk // 2), BF16),
        vm((width // groups, chunk // 2), F32),
        vm((width // groups, chunk // 2), F32),
        vm((8, 128), F32),
        vm((columns, 8, 128), F32),
        vm((8, 128), F32),
        vm((groups, 8, 128), F32),
        dma((5,)),
        dma((2 * columns + 2,)),
        dma((2 * columns,)),
        dma((2 * groups,)),
        dma((2 * groups,)),
    ] + [dma((2, groups) if i in (10, 11, 12, 13) else (groups,)) for i in range(18)] + [dma((2,))]
    anywhere = pl.BlockSpec(memory_space=pl.ANY)
    vmem = pl.BlockSpec(memory_space=pltpu.VMEM)
    loss, student_gradient, projector_gradient = pl.pallas_call(
        functools.partial(kernel, groups, columns),
        out_shape=(
            jax.ShapeDtypeStruct((1, 1), F32),
            jax.ShapeDtypeStruct((rows, width), BF16),
            jax.ShapeDtypeStruct((width // groups, wide // columns), F32),
        ),
        in_specs=[anywhere] * 4 + [vmem] * 4,
        out_specs=(pl.BlockSpec(memory_space=pltpu.SMEM), vmem, vmem),
        scratch_shapes=scratch,
        compiler_params=pltpu.CompilerParams(
            collective_id=0, has_side_effects=True, vmem_limit_bytes=58 * 1024 * 1024
        ),
        cost_estimate=pl.CostEstimate(
            flops=12_000_000_000, bytes_accessed=16_000_000, transcendentals=1_000_000
        ),
    )(
        student,
        teacher,
        teacher_similarity,
        projector,
        hard_group.T,
        hard_local.T,
        hard_count.reshape(1, rows),
        text_weight.reshape(1, rows),
    )
    return loss.reshape(()), student_gradient, projector_gradient


def solution(mesh):
    return jax.shard_map(
        local_program,
        mesh=mesh,
        in_specs=(
            P(("group", "dp"), None),
            P(("group", "dp"), None),
            P(("group", "dp"), None),
            P(),
            P(("group", "dp"), None),
            P(("group", "dp"), None),
            P(("group", "dp")),
            P(("group", "dp")),
        ),
        out_specs=(P(), P(("group", "dp"), None), P("group", "dp")),
        check_vma=False,
    )
```

```python
import functools
import jax
import jax.numpy as jnp
from jax import lax
from jax.experimental import pallas as pl
from jax.experimental.pallas import tpu as pltpu
from jax.sharding import PartitionSpec as P

HARD = 2
EPSILON = 1e-06
INVERSE_TEMP = 20.0
SIMILARITY_COEF = 200.0
HARD_WEIGHT = 20.0
LOSS_SCALE = 1024.0
MESH = pl.DeviceIdType.MESH
F32 = jnp.float32
BF16 = jnp.bfloat16


def dot(left, right):
    return jnp.dot(left, right, preferred_element_type=F32)


def dot_t(left, right):
    return lax.dot_general(left, right, (((1,), (1,)), ((), ())), preferred_element_type=F32)


def loop(low, high, body):
    def step(i, carry):
        body(i)
        return carry

    lax.fori_loop(low, high, step, 0)


def kernel(
    groups,
    columns,
    student,
    teacher,
    sims,
    projector,
    hard_group_in,
    hard_local_in,
    hard_count_in,
    text_weight_in,
    loss_out,
    student_out,
    projector_out,
    hard_group,
    hard_local,
    hard_count,
    text_weight,
    student_made,
    s_set,
    s_col,
    s_turned,
    c_turned,
    proj,
    teach,
    sim_t,
    unit_t,
    cols_t,
    sim_s,
    exp_s,
    exp_t,
    cross_s,
    row_total,
    h_mat,
    w_mat,
    back,
    comb,
    pair_rows,
    grad,
    grad_cols,
    facts,
    facts_set,
    facts_col,
    part,
    parts,
    hard_sum,
    totals,
    totals_set,
    within,
    arrived,
    mirror_out,
    mirror_in,
    loss_tile,
    loss_set,
    loss_tile2,
    loss_col,
    local_sem,
    set_send,
    set_recv,
    col_send,
    col_recv,
    unit_send,
    unit_recv,
    fset_send,
    fset_recv,
    fcol_send,
    fcol_recv,
    part_send,
    part_recv,
    tot_send,
    tot_recv,
    grad_send,
    grad_recv,
    out_send,
    out_recv,
    lset_send,
    lset_recv,
    lcol_send,
    lcol_recv,
    mirror_sem,
):
    rows, width = student.shape
    chunk = unit_t.shape[2]
    count = unit_t.shape[0]
    half = rows // 2
    set_count = rows * columns
    g = lax.axis_index("group")
    d = lax.axis_index("dp")
    xs, zs = groups // 4, columns // 2
    x, yh, core = g // 4, lax.rem(g // 2, 2), lax.rem(g, 2)
    yl, z = d // zs, lax.rem(d, zs)

    def flip(value, by):
        return 1 - value if by else value

    def col_id(dx, fy, fc):
        return lax.rem(x + dx % xs, xs) * 4 + flip(yh, fy) * 2 + flip(core, fc)

    def set_id(fy, dz):
        return flip(yl, fy) * zs + lax.rem(z + dz % zs, zs)

    def rows_of(block):
        return pl.ds(pl.multiple_of(block * rows, rows), rows)

    def lanes_of(block):
        return pl.ds(pl.multiple_of(block * rows, rows), rows)

    def chunk_of(q):
        return pl.ds(pl.multiple_of(q * chunk, chunk), chunk)

    def copy(src, dst, send, recv, group, column):
        return pltpu.make_async_remote_copy(
            src_ref=src,
            dst_ref=dst,
            send_sem=send,
            recv_sem=recv,
            device_id=(group, column),
            device_id_type=MESH,
        )

    local = [
        pltpu.make_async_copy(student, s_set.at[rows_of(d)], local_sem.at[0]),
        pltpu.make_async_copy(student, s_col.at[rows_of(g)], local_sem.at[1]),
        pltpu.make_async_copy(teacher, teach, local_sem.at[2]),
        pltpu.make_async_copy(projector, proj, local_sem.at[3]),
        pltpu.make_async_copy(sims, sim_t, local_sem.at[4]),
        pltpu.make_async_copy(hard_group_in, hard_group, local_sem.at[5]),
        pltpu.make_async_copy(hard_local_in, hard_local, local_sem.at[6]),
        pltpu.make_async_copy(hard_count_in, hard_count, local_sem.at[7]),
        pltpu.make_async_copy(text_weight_in, text_weight, local_sem.at[8]),
    ]
    for one in (2, 0, 1, 3, 4, 5, 6, 7, 8):
        local[one].start()

    barrier = pltpu.get_barrier_semaphore()

    def greet(o):
        pl.semaphore_signal(
            barrier, inc=1, device_id=(g, lax.rem(d + o, columns)), device_id_type=MESH
        )
        pl.semaphore_signal(
            barrier, inc=1, device_id=(lax.rem(g + o, groups), d), device_id_type=MESH
        )

    loop(1, columns, greet)

    @pl.when(g != d)
    def greet_mirror():
        pl.semaphore_signal(barrier, inc=1, device_id=(d, g), device_id_type=MESH)

    local[2].wait()

    def square_sum(q, total):
        t = teach[:, chunk_of(q)].astype(F32)
        t = t * t
        return total + sum(t[:, i : i + 128] for i in range(0, chunk, 128))

    t_total = lax.fori_loop(0, count, square_sum, jnp.zeros((rows, 128), F32))
    t_scale = 1.0 / jnp.sqrt(jnp.sum(t_total, 1, keepdims=True) + EPSILON)

    def make_unit(q):
        unit_t[q] = (teach[:, chunk_of(q)].astype(F32) * t_scale).astype(BF16)

    loop(0, count, make_unit)
    others = (lax.rem(g - d + groups, groups) + groups - 1) // groups
    pl.semaphore_wait(barrier, 2 * (columns - 1) + others)

    pending = []

    def region(ref, block, part_of):
        start = pl.multiple_of(block * rows, rows)
        if part_of is None:
            return ref.at[pl.ds(start, rows)]
        return ref.at[pl.ds(pl.multiple_of(start + part_of * half, half), half)]

    def set_slot(fy, dz, part_of):
        return (fy * zs + dz % zs) * 2 + (part_of or 0)

    def send_set(fy, dz, to_fy, to_dz, part_of=None):
        block = set_id(fy, dz)
        place = region(s_set, block, part_of)
        source = student if (fy == 0 and dz == 0) else place
        one = copy(
            source,
            place,
            set_send.at[len([p for p in pending if p[0] == "set"])],
            set_recv.at[set_slot(fy ^ to_fy, dz - to_dz, part_of)],
            g,
            set_id(to_fy, to_dz),
        )
        one.start()
        pending.append(("set", one))

    def wait_set(fy, dz, part_of=None):
        place = region(s_set, set_id(fy, dz), part_of)
        slot = set_slot(fy, dz, part_of)
        copy(place, place, set_send.at[0], set_recv.at[slot], g, set_id(1, 0)).wait_recv()

    def col_slot(dx, fy, fc, part_of):
        return ((fy * 2 + fc) * xs + dx % xs) * 2 + (part_of or 0)

    def send_col(dx, fy, to_dx, to_fy, to_fc, part_of=None):
        block = col_id(dx, fy, 0)
        place = region(s_col, block, part_of)
        source = student if (fy == 0 and dx == 0) else place
        one = copy(
            source,
            place,
            col_send.at[len([p for p in pending if p[0] == "col"])],
            col_recv.at[col_slot(dx - to_dx, fy ^ to_fy, to_fc, part_of)],
            col_id(to_dx, to_fy, to_fc),
            d,
        )
        one.start()
        pending.append(("col", one))

    def wait_col(dx, fy, fc, part_of=None):
        place = region(s_col, col_id(dx, fy, fc), part_of)
        slot = col_slot(dx, fy, fc, part_of)
        copy(place, place, col_send.at[0], col_recv.at[slot], col_id(0, 0, 1), d).wait_recv()

    send_set(0, 0, 1, 0)
    send_set(0, 0, 0, 1)
    send_set(0, 0, 0, -1)
    send_col(0, 0, 0, 1, 0)
    send_col(0, 0, 1, 0, 0)
    send_col(0, 0, -1, 0, 0)
    send_col(0, 0, 0, 0, 1)

    def pass_set(step):
        if step == 0:
            wait_set(1, 0)
            send_set(1, 0, 0, 1)
            send_set(1, 0, 0, -1)
            return
        last = step == zs // 2 - 1
        for fy in (0, 1):
            wait_set(fy, -step)
            send_set(fy, -step, 0, 1, 0 if last else None)
            wait_set(fy, step)
            send_set(fy, step, 0, -1, 1 if last else None)

    def pass_col(step):
        if step == 0:
            wait_col(0, 1, 0)
            send_col(0, 1, 1, 0, 0)
            send_col(0, 1, -1, 0, 0)
            send_col(0, 1, 0, 0, 1)
        elif step == 1:
            for fy in (0, 1):
                wait_col(-1, fy, 0)
                send_col(-1, fy, 1, 0, 0, 0)
                send_col(-1, fy, 0, 0, 1)
                wait_col(1, fy, 0)
                send_col(1, fy, -1, 0, 0, 1)
                send_col(1, fy, 0, 0, 1)
        else:
            for fy in (0, 1):
                wait_col(2, fy, 0, 0)
                wait_col(2, fy, 0, 1)
                send_col(2, fy, 0, 0, 1)

    def exchange(src_of, dst, send, recv, along):
        me, size = (d, columns) if along == "dp" else (g, groups)

        def at(o):
            peer = lax.rem(me + o, size)
            where = (g, peer) if along == "dp" else (peer, d)
            return copy(src_of(peer), dst(me), send.at[o], recv.at[o], *where)

        def arrive(o):
            source = lax.rem(me + size - o, size)
            where = (g, source) if along == "dp" else (source, d)
            copy(dst(source), dst(source), send.at[o], recv.at[o], *where).wait_recv()

        return (
            lambda: loop(1, size, lambda o: at(lax.rem(5 * o, size)).start()),
            lambda: loop(1, size, arrive),
            lambda: loop(1, size, lambda o: at(o).wait_send()),
        )

    unit_start, unit_wait, unit_end = exchange(
        lambda peer: unit_t.at[peer], lambda me: cols_t.at[rows_of(me)], unit_send, unit_recv, "group"
    )
    unit_start()
    cols_t[rows_of(g)] = unit_t[g]

    local[0].wait()
    local[1].wait()
    local[3].wait()
    back[...] = jnp.zeros_like(back)

    def project(q, carry):
        squares, along = carry
        p = dot(s_set[rows_of(d)], proj[:, chunk_of(q)])
        both = p * unit_t[q].astype(F32)
        back[...] += dot_t(p.astype(BF16), proj[:, chunk_of(q)])
        for i in range(0, chunk, 128):
            piece = p[:, i : i + 128]
            squares = squares + piece * piece
            along = along + both[:, i : i + 128]
        return squares, along

    zero = jnp.zeros((rows, 128), F32)
    squares, along = lax.fori_loop(0, count, project, (zero, zero))
    norm = jnp.sqrt(jnp.sum(squares, 1, keepdims=True) + EPSILON)
    cosine = jnp.sum(along, 1, keepdims=True)
    inverse = 1.0 / norm

    def split_store(value):
        high = value.astype(BF16)
        pair_rows[0:rows] = high
        pair_rows[rows : 2 * rows] = (value - high.astype(F32)).astype(BF16)

    split_store(back[...] * inverse)
    pass_set(0)

    sub = lax.broadcasted_iota(jnp.int32, (rows, rows), 0)
    lane = lax.broadcasted_iota(jnp.int32, (rows, rows), 1)
    eye = sub == lane

    def to_row(column):
        return jnp.sum(jnp.where(eye, column, 0.0), 0, keepdims=True)

    def to_column(row):
        return jnp.sum(jnp.where(eye, row, 0.0), 1, keepdims=True)

    for one in range(4, 9):
        local[one].wait()

    def teacher_exp(b, total):
        value = jnp.exp(sim_t[:, lanes_of(b)] * INVERSE_TEMP)
        value = jnp.where(jnp.logical_and(eye, b == d), 0.0, value)
        exp_t[b] = value
        return total + value

    total_t = jnp.sum(lax.fori_loop(0, columns, teacher_exp, zero), 1, keepdims=True)
    weight_row = text_weight[...]
    used = hard_count[...]
    facts[0:1, :] = to_row(inverse)
    facts[1:2, :] = to_row(1.0 / total_t)
    facts[2:3, :] = weight_row
    for k in range(HARD):
        facts[3 + k : 4 + k, :] = (
            hard_group[k : k + 1, :] * rows + hard_local[k : k + 1, :]
        ).astype(F32)
        facts[5 + k : 6 + k, :] = (
            jnp.where(used > k, HARD_WEIGHT / used.astype(F32), 0.0) * weight_row
        )
    facts[7:8, :] = jnp.zeros((1, rows), F32)
    facts_set[d] = facts[...]
    facts_col[g] = facts[...]
    fcol_start, fcol_wait, fcol_end = exchange(
        lambda peer: facts, lambda me: facts_col.at[me], fcol_send, fcol_recv, "group"
    )
    fset_start, fset_wait, fset_end = exchange(
        lambda peer: facts, lambda me: facts_set.at[me], fset_send, fset_recv, "dp"
    )
    fcol_start()
    fset_start()
    pass_set(1)
    pass_col(0)

    row_total[...] = zero

    def multiply(block):
        both = dot_t(pair_rows[...], s_set[rows_of(block)])
        sim_s[block] = both[0:rows] + both[rows : 2 * rows]
        s_turned[:, lanes_of(block)] = s_set[rows_of(block)].T

    def finish(block):
        value = sim_s[block] * facts_set[block, 0:1, :]
        grown = jnp.exp(value * INVERSE_TEMP)
        grown = jnp.where(jnp.logical_and(eye, block == d), 0.0, grown)
        sim_s[block] = value
        exp_s[block] = grown
        row_total[...] += grown

    for fy, dz in ((0, 0), (1, 0), (0, -1), (0, 1), (1, -1), (1, 1)):
        multiply(set_id(fy, dz))
    pass_set(2)
    pass_col(1)
    for fy, dz in ((0, -2), (0, 2), (1, -2), (1, 2)):
        multiply(set_id(fy, dz))

    unit_wait()
    fcol_wait()
    numbers = lax.broadcasted_iota(jnp.int32, (rows, 2 * rows), 0).astype(F32)
    step_blocks = 4

    def pick(b):
        queries = cols_t[pl.ds(pl.multiple_of(2 * b * rows, 2 * rows), 2 * rows)]
        first, second = [
            jnp.concatenate([facts_col[2 * b + i, 3 + k : 4 + k, :] for i in (0, 1)], 1)
            for k in range(HARD)
        ]
        sums = [jnp.zeros((1, 2 * rows), F32)] * HARD
        for c in range(0, groups, step_blocks):
            gram = dot_t(cols_t[c * rows : (c + step_blocks) * rows], queries)
            for j in range(step_blocks):
                low = float((c + j) * rows)
                here = jnp.logical_and(first >= low, first < low + rows)
                wanted = jnp.where(here, first, second) - low
                found = jnp.sum(
                    jnp.where(numbers == wanted, gram[j * rows : (j + 1) * rows], 0.0),
                    0,
                    keepdims=True,
                )
                sums[0] = sums[0] + jnp.where(here, found, 0.0)
                sums[1] = sums[1] + jnp.where(here, 0.0, found)
        for k in range(HARD):
            for i in (0, 1):
                part[pl.ds(k * groups + 2 * b + i, 1), :] = sums[k][:, i * rows : (i + 1) * rows]

    loop(0, groups // 4, pick)
    pass_set(3)
    pass_col(2)
    loop(groups // 4, groups // 2, pick)
    part_start, part_wait, part_end = exchange(
        lambda peer: part, lambda me: parts.at[me], part_send, part_recv, "group"
    )
    part_start()
    parts[g] = part[...]
    for fy, dz in ((0, -3), (0, 3), (1, -3), (1, 3)):
        multiply(set_id(fy, dz))
    fset_wait()

    def finish_near(i):
        fy, dz = i // (zs - 1), lax.rem(i, zs - 1) - (zs // 2 - 1)
        finish((yl + fy - 2 * fy * yl) * zs + lax.rem(z + dz + zs, zs))

    loop(0, 2 * (zs - 1), finish_near)
    for dx in range(xs):
        for fy in (0, 1):
            wait_col(dx, fy, 1)

    def cross_pair(b):
        both = dot_t(
            pair_rows[...], s_col[pl.ds(pl.multiple_of(2 * b * rows, 2 * rows), 2 * rows)]
        )
        value = both[0:rows] + both[rows : 2 * rows]
        for i in (0, 1):
            cross_s[2 * b + i] = (
                value[:, i * rows : (i + 1) * rows] * facts_col[2 * b + i, 0:1, :]
            )

    loop(0, groups // 2, cross_pair)
    for fy in (0, 1):
        wait_set(fy, zs // 2, 0)
        wait_set(fy, zs // 2, 1)
        far = set_id(fy, zs // 2)
        multiply(far)
        finish(far)
    total_s = jnp.sum(row_total[...], 1, keepdims=True)
    totals[...] = jnp.broadcast_to(to_row(1.0 / total_s), totals.shape)
    totals_set[d] = totals[...]
    tot_start, tot_wait, tot_end = exchange(
        lambda peer: totals, lambda me: totals_set.at[me], tot_send, tot_recv, "dp"
    )
    tot_start()

    part_wait()
    hard_sum[...] = jnp.sum(parts[...], 0)
    weight = to_column(weight_row)
    own_hard = [to_column(hard_sum[pl.ds(k * groups + g, 1), :]) for k in range(HARD)]
    own_target = [to_column(facts[3 + k : 4 + k, :]) for k in range(HARD)]
    own_entry = [to_column(facts[5 + k : 6 + k, :]) for k in range(HARD)]
    own_ids = sub.astype(F32) + (g * rows).astype(F32)
    lane_ids = lane.astype(F32)

    def hard(b, loss):
        scale = facts_col[b, 0:1, :]
        cross = cross_s[b]
        ids = lane_ids + (b * rows).astype(F32)
        value = jnp.zeros_like(cross)
        for k in range(HARD):
            asked = jnp.where(ids == own_target[k], own_entry[k], 0.0)
            difference = cross - own_hard[k]
            term = asked * difference
            loss = loss + term * difference
            listed = jnp.where(
                facts_col[b, 3 + k : 4 + k, :] == own_ids, facts_col[b, 5 + k : 6 + k, :], 0.0
            )
            value = value + term + listed * (cross - hard_sum[pl.ds(k * groups + b, 1), :])
        h_mat[:, lanes_of(b)] = (2.0 * scale * value).astype(BF16)
        return loss

    hard_loss = lax.fori_loop(0, groups, hard, zero)
    piece = 256 if width >= 256 else width
    for n in range(0, width, piece):
        comb[:, n : n + piece] = dot(h_mat[...], s_col[:, n : n + piece])
    scale_s, scale_t = weight / total_s, weight / total_t

    def pairs(b, carry):
        squares, divergence = carry
        gap = sim_s[b] - sim_t[:, lanes_of(b)]
        their = facts_set[b, 2:3, :]
        grown = exp_t[b]
        sim_s[b] = (2.0 * SIMILARITY_COEF / set_count) * gap * (
            weight + their
        ) + INVERSE_TEMP * (exp_s[b] * scale_s - grown * (scale_t + their * facts_set[b, 1:2, :]))
        return squares + gap * gap, divergence + grown * gap

    squares, divergence = lax.fori_loop(0, columns, pairs, (zero, zero))
    tot_wait()

    def complete(b):
        their = INVERSE_TEMP * facts_set[b, 2:3, :] * totals_set[b, 0:1, :]
        w_mat[:, lanes_of(b)] = (
            (sim_s[b] + exp_s[b] * their) * facts_set[b, 0:1, :]
        ).astype(BF16)

    loop(0, columns, complete)
    for n in range(0, width, piece):
        comb[:, n : n + piece] += dot(w_mat[...], s_set[:, n : n + piece])
    combined = comb[...] * LOSS_SCALE
    inner = jnp.sum(back[...] * combined, 1, keepdims=True) - LOSS_SCALE * weight * cosine
    split_store(
        combined * inverse
        - s_set[rows_of(d)].astype(F32) * (inner * inverse * inverse * inverse)
    )
    thin = chunk // 2
    teacher_scale = LOSS_SCALE * weight * inverse

    def gradient(q):
        both = dot(pair_rows[...], proj[:, chunk_of(q)])
        value = both[0:rows] + both[rows : 2 * rows] - teacher_scale * unit_t[q].astype(F32)
        for h in (0, 1):
            grad[h, q] = value[:, h * thin : (h + 1) * thin].astype(BF16)

    def set_copy(o):
        peer = lax.rem(d + o, columns)
        return copy(
            grad.at[0, peer],
            grad_cols.at[0, rows_of(d)],
            grad_send.at[0, o],
            grad_recv.at[0, o],
            g,
            peer,
        )

    def col_copy(o):
        peer = lax.rem(g + o, groups)
        return copy(
            grad.at[1, peer],
            grad_cols.at[1, rows_of(g)],
            grad_send.at[1, o],
            grad_recv.at[1, o],
            peer,
            d,
        )

    def gradient_step(o):
        turn = lax.rem(5 * o, columns)
        q = lax.rem(d + turn, columns)
        gradient(q)
        apart = lax.rem(q + groups - g, groups)

        @pl.when(apart != 0)
        def send_col_part():
            col_copy(apart).start()

        @pl.when(o != columns)
        def send_set_part():
            set_copy(turn).start()

    loop(1, columns + 1, gradient_step)
    grad_cols[0, rows_of(d)] = grad[0, d]
    grad_cols[1, rows_of(g)] = grad[1, g]

    sim_term = (SIMILARITY_COEF / set_count) * jnp.sum(squares, 1, keepdims=True)
    kl_term = (
        jnp.log(total_s)
        - jnp.log(total_t)
        - INVERSE_TEMP * jnp.sum(divergence, 1, keepdims=True) / total_t
    )
    per_text = weight * (1.0 - cosine * inverse + sim_term + kl_term) + jnp.sum(
        hard_loss, 1, keepdims=True
    )
    loss_tile[...] = jnp.broadcast_to(jnp.sum(per_text, 0, keepdims=True), loss_tile.shape)
    loss_set[d] = loss_tile[...]
    lset_start, lset_wait, lset_end = exchange(
        lambda peer: loss_tile, lambda me: loss_set.at[me], lset_send, lset_recv, "dp"
    )
    lset_start()

    def turn_col(b):
        c_turned[:, lanes_of(b)] = s_col[rows_of(b)].T

    loop(0, groups, turn_col)

    def set_arrive(o):
        source = lax.rem(d + columns - o, columns)
        place = grad_cols.at[0, rows_of(source)]
        copy(place, place, grad_send.at[0, o], grad_recv.at[0, o], g, source).wait_recv()

    def col_arrive(o):
        source = lax.rem(g + groups - o, groups)
        place = grad_cols.at[1, rows_of(source)]
        copy(place, place, grad_send.at[1, o], grad_recv.at[1, o], source, d).wait_recv()

    share = width // groups

    def products(h, turned):
        for n in range(0, width, piece):
            result = dot(turned[n : n + piece, :], grad_cols[h]).astype(BF16)
            for i in range(piece // share):
                within[h, n // share + i] = result[i * share : (i + 1) * share]

    def out_exchange(h, along):
        return exchange(
            lambda peer: within.at[h, peer],
            lambda me: arrived.at[h, me],
            out_send.at[h],
            out_recv.at[h],
            along,
        )

    loop(1, groups, col_arrive)
    products(1, c_turned)
    out1_start, out1_wait, out1_end = out_exchange(1, "dp")
    out1_start()
    arrived[1, d] = within[1, d]

    comb[...] = jnp.zeros_like(comb)

    def student_part(q):
        both = jnp.concatenate([grad[0, q], grad[1, q]], 1)
        comb[...] += dot_t(both, proj[:, chunk_of(q)])

    loop(0, count, student_part)
    student_made[...] = comb[...].astype(BF16)
    student_copy = pltpu.make_async_copy(student_made, student_out, local_sem.at[9])
    student_copy.start()

    for _, one in pending:
        one.wait_send()
    for end in (unit_end, fcol_end, fset_end, part_end, tot_end):
        end()
    lset_wait()
    loss_tile2[...] = jnp.sum(loss_set[...], 0)
    loss_col[g] = loss_tile2[...]
    lcol_start, lcol_wait, lcol_end = exchange(
        lambda peer: loss_tile2, lambda me: loss_col.at[me], lcol_send, lcol_recv, "group"
    )
    lcol_start()

    loop(1, columns, set_arrive)
    products(0, s_turned)
    out0_start, out0_wait, out0_end = out_exchange(0, "group")
    out0_start()
    arrived[0, g] = within[0, g]
    out1_wait()
    mirror_out[...] = jnp.sum(arrived[1].astype(F32), 0)
    mirror = copy(mirror_out, mirror_in, mirror_sem.at[0], mirror_sem.at[1], d, g)

    @pl.when(g != d)
    def send_mirror():
        mirror.start()

    lcol_wait()
    loss_out[0, 0] = jnp.sum(loss_col[...]) * (
        1.0 / (8.0 * 128.0 * rows * groups * columns)
    )
    loop(1, columns, lambda o: set_copy(o).wait_send())
    loop(1, groups, lambda o: col_copy(o).wait_send())
    for end in (lset_end, lcol_end, out1_end):
        end()
    out0_wait()
    projector_out[:, :thin] = jnp.sum(arrived[0].astype(F32), 0)

    @pl.when(g != d)
    def take_mirror():
        mirror.wait()
        projector_out[:, thin:] = mirror_in[...]

    @pl.when(g == d)
    def keep_own():
        projector_out[:, thin:] = mirror_out[...]

    out0_end()
    student_copy.wait()


def local_program(
    student, teacher, teacher_similarity, projector, hard_group, hard_local, hard_count, text_weight
):
    rows, width = student.shape
    groups = lax.axis_size("group")
    columns = lax.axis_size("dp")
    wide = projector.shape[1]
    chunk = wide // groups
    dma = pltpu.SemaphoreType.DMA
    vm = pltpu.VMEM
    texts, col_texts = rows * columns, rows * groups
    scratch = [
        vm((HARD, rows), jnp.int32),
        vm((HARD, rows), jnp.int32),
        vm((1, rows), jnp.int32),
        vm((1, rows), F32),
        vm((rows, width), BF16),
        vm((texts, width), BF16),
        vm((col_texts, width), BF16),
        vm((width, texts), BF16),
        vm((width, col_texts), BF16),
        vm((width, wide), BF16),
        vm((rows, wide), BF16),
        vm((rows, texts), F32),
        vm((groups, rows, chunk), BF16),
        vm((col_texts, chunk), BF16),
        vm((columns, rows, rows), F32),
        vm((columns, rows, rows), F32),
        vm((columns, rows, rows), F32),
        vm((groups, rows, rows), F32),
        vm((rows, rows), F32),
        vm((rows, col_texts), BF16),
        vm((rows, texts), BF16),
        vm((rows, width), F32),
        vm((rows, width), F32),
        vm((2 * rows, width), BF16),
        vm((2, columns, rows, chunk // 2), BF16),
        vm((2, texts, chunk // 2), BF16),
        vm((8, rows), F32),
        vm((columns, 8, rows), F32),
        vm((groups, 8, rows), F32),
        vm((HARD * groups, rows), F32),
        vm((groups, HARD * groups, rows), F32),
        vm((HARD * groups, rows), F32),
        vm((8, rows), F32),
        vm((columns, 8, rows), F32),
        vm((2, groups, width // groups, chunk // 2), BF16),
        vm((2, groups, width // groups, chunk // 2), BF16),
        vm((width // groups, chunk // 2), F32),
        vm((width // groups, chunk // 2), F32),
        vm((8, 128), F32),
        vm((columns, 8, 128), F32),
        vm((8, 128), F32),
        vm((groups, 8, 128), F32),
        dma((10,)),
        dma((2 * columns + 2,)),
        dma((2 * columns,)),
        dma((2 * groups,)),
        dma((2 * groups,)),
    ] + [dma((2, groups) if i in (10, 11, 12, 13) else (groups,)) for i in range(18)] + [dma((2,))]
    anywhere = pl.BlockSpec(memory_space=pl.ANY)
    vmem = pl.BlockSpec(memory_space=pltpu.VMEM)
    loss, student_gradient, projector_gradient = pl.pallas_call(
        functools.partial(kernel, groups, columns),
        out_shape=(
            jax.ShapeDtypeStruct((1, 1), F32),
            jax.ShapeDtypeStruct((rows, width), BF16),
            jax.ShapeDtypeStruct((width // groups, wide // columns), F32),
        ),
        in_specs=[anywhere] * 8,
        out_specs=(pl.BlockSpec(memory_space=pltpu.SMEM), anywhere, vmem),
        scratch_shapes=scratch,
        compiler_params=pltpu.CompilerParams(
            collective_id=0, has_side_effects=True, vmem_limit_bytes=58 * 1024 * 1024
        ),
        cost_estimate=pl.CostEstimate(
            flops=12_000_000_000, bytes_accessed=16_000_000, transcendentals=1_000_000
        ),
    )(
        student,
        teacher,
        teacher_similarity,
        projector,
        hard_group.T,
        hard_local.T,
        hard_count.reshape(1, rows),
        text_weight.reshape(1, rows),
    )
    return loss.reshape(()), student_gradient, projector_gradient


def solution(mesh):
    return jax.shard_map(
        local_program,
        mesh=mesh,
        in_specs=(
            P(("group", "dp"), None),
            P(("group", "dp"), None),
            P(("group", "dp"), None),
            P(),
            P(("group", "dp"), None),
            P(("group", "dp"), None),
            P(("group", "dp")),
            P(("group", "dp")),
        ),
        out_specs=(P(), P(("group", "dp"), None), P("group", "dp")),
        check_vma=False,
    )
```

```python
import functools
import jax
import jax.numpy as jnp
from jax import lax
from jax.experimental import pallas as pl
from jax.experimental.pallas import tpu as pltpu
from jax.sharding import PartitionSpec as P

HARD = 2
EPSILON = 1e-06
INVERSE_TEMP = 20.0
SIMILARITY_COEF = 200.0
HARD_WEIGHT = 20.0
LOSS_SCALE = 1024.0
MESH = pl.DeviceIdType.MESH
F32 = jnp.float32
BF16 = jnp.bfloat16


def dot(left, right):
    return jnp.dot(left, right, preferred_element_type=F32)


def dot_t(left, right):
    return lax.dot_general(left, right, (((1,), (1,)), ((), ())), preferred_element_type=F32)


def loop(low, high, body):
    def step(i, carry):
        body(i)
        return carry

    lax.fori_loop(low, high, step, 0)


def kernel(
    groups,
    columns,
    student,
    teacher,
    sims,
    projector,
    hard_group_in,
    hard_local_in,
    hard_count_in,
    text_weight_in,
    loss_out,
    student_out,
    projector_out,
    hard_group,
    hard_local,
    hard_count,
    text_weight,
    student_made,
    s_set,
    s_col,
    s_turned,
    c_turned,
    proj,
    teach,
    sim_t,
    unit_t,
    cols_t,
    sim_s,
    exp_s,
    exp_t,
    cross_s,
    row_total,
    h_mat,
    w_mat,
    back,
    comb,
    pair_rows,
    grad,
    grad_cols,
    facts,
    facts_set,
    facts_col,
    part,
    parts,
    hard_sum,
    totals,
    totals_set,
    within,
    arrived,
    mirror_out,
    mirror_in,
    loss_tile,
    loss_set,
    loss_tile2,
    loss_col,
    local_sem,
    set_send,
    set_recv,
    col_send,
    col_recv,
    unit_send,
    unit_recv,
    fset_send,
    fset_recv,
    fcol_send,
    fcol_recv,
    part_send,
    part_recv,
    tot_send,
    tot_recv,
    grad_send,
    grad_recv,
    out_send,
    out_recv,
    lset_send,
    lset_recv,
    lcol_send,
    lcol_recv,
    mirror_sem,
):
    rows, width = student.shape
    chunk = unit_t.shape[2]
    count = unit_t.shape[0]
    half = rows // 2
    set_count = rows * columns
    g = lax.axis_index("group")
    d = lax.axis_index("dp")
    xs, zs = groups // 4, columns // 2
    x, yh, core = g // 4, lax.rem(g // 2, 2), lax.rem(g, 2)
    yl, z = d // zs, lax.rem(d, zs)

    def flip(value, by):
        return 1 - value if by else value

    def col_id(dx, fy, fc):
        return lax.rem(x + dx % xs, xs) * 4 + flip(yh, fy) * 2 + flip(core, fc)

    def set_id(fy, dz):
        return flip(yl, fy) * zs + lax.rem(z + dz % zs, zs)

    def rows_of(block):
        return pl.ds(pl.multiple_of(block * rows, rows), rows)

    def lanes_of(block):
        return pl.ds(pl.multiple_of(block * rows, rows), rows)

    def chunk_of(q):
        return pl.ds(pl.multiple_of(q * chunk, chunk), chunk)

    def copy(src, dst, send, recv, group, column):
        return pltpu.make_async_remote_copy(
            src_ref=src,
            dst_ref=dst,
            send_sem=send,
            recv_sem=recv,
            device_id=(group, column),
            device_id_type=MESH,
        )

    barrier = pltpu.get_barrier_semaphore()

    def greet(o):
        pl.semaphore_signal(
            barrier, inc=1, device_id=(g, lax.rem(d + o, columns)), device_id_type=MESH
        )
        pl.semaphore_signal(
            barrier, inc=1, device_id=(lax.rem(g + o, groups), d), device_id_type=MESH
        )

    loop(1, columns, greet)

    @pl.when(g != d)
    def greet_mirror():
        pl.semaphore_signal(barrier, inc=1, device_id=(d, g), device_id_type=MESH)

    local = [
        pltpu.make_async_copy(student, s_set.at[rows_of(d)], local_sem.at[0]),
        pltpu.make_async_copy(student, s_col.at[rows_of(g)], local_sem.at[1]),
        pltpu.make_async_copy(teacher, teach, local_sem.at[2]),
        pltpu.make_async_copy(projector, proj, local_sem.at[3]),
        pltpu.make_async_copy(sims, sim_t, local_sem.at[4]),
        pltpu.make_async_copy(hard_group_in, hard_group, local_sem.at[5]),
        pltpu.make_async_copy(hard_local_in, hard_local, local_sem.at[6]),
        pltpu.make_async_copy(hard_count_in, hard_count, local_sem.at[7]),
        pltpu.make_async_copy(text_weight_in, text_weight, local_sem.at[8]),
    ]
    for one in (2, 0, 1, 3, 4, 5, 6, 7, 8):
        local[one].start()

    local[2].wait()

    def square_sum(q, total):
        t = teach[:, chunk_of(q)].astype(F32)
        t = t * t
        return total + sum(t[:, i : i + 128] for i in range(0, chunk, 128))

    t_total = lax.fori_loop(0, count, square_sum, jnp.zeros((rows, 128), F32))
    t_scale = 1.0 / jnp.sqrt(jnp.sum(t_total, 1, keepdims=True) + EPSILON)

    def make_unit(q):
        unit_t[q] = (teach[:, chunk_of(q)].astype(F32) * t_scale).astype(BF16)

    loop(0, count, make_unit)
    others = (lax.rem(g - d + groups, groups) + groups - 1) // groups
    pl.semaphore_wait(barrier, 2 * (columns - 1) + others)

    pending = []

    def region(ref, block, part_of):
        start = pl.multiple_of(block * rows, rows)
        if part_of is None:
            return ref.at[pl.ds(start, rows)]
        return ref.at[pl.ds(pl.multiple_of(start + part_of * half, half), half)]

    def set_slot(fy, dz, part_of):
        return (fy * zs + dz % zs) * 2 + (part_of or 0)

    def send_set(fy, dz, to_fy, to_dz, part_of=None):
        block = set_id(fy, dz)
        place = region(s_set, block, part_of)
        source = student if (fy == 0 and dz == 0) else place
        one = copy(
            source,
            place,
            set_send.at[len([p for p in pending if p[0] == "set"])],
            set_recv.at[set_slot(fy ^ to_fy, dz - to_dz, part_of)],
            g,
            set_id(to_fy, to_dz),
        )
        one.start()
        pending.append(("set", one))

    def wait_set(fy, dz, part_of=None):
        place = region(s_set, set_id(fy, dz), part_of)
        slot = set_slot(fy, dz, part_of)
        copy(place, place, set_send.at[0], set_recv.at[slot], g, set_id(1, 0)).wait_recv()

    def col_slot(dx, fy, fc, part_of):
        return ((fy * 2 + fc) * xs + dx % xs) * 2 + (part_of or 0)

    def send_col(dx, fy, to_dx, to_fy, to_fc, part_of=None):
        block = col_id(dx, fy, 0)
        place = region(s_col, block, part_of)
        source = student if (fy == 0 and dx == 0) else place
        one = copy(
            source,
            place,
            col_send.at[len([p for p in pending if p[0] == "col"])],
            col_recv.at[col_slot(dx - to_dx, fy ^ to_fy, to_fc, part_of)],
            col_id(to_dx, to_fy, to_fc),
            d,
        )
        one.start()
        pending.append(("col", one))

    def wait_col(dx, fy, fc, part_of=None):
        place = region(s_col, col_id(dx, fy, fc), part_of)
        slot = col_slot(dx, fy, fc, part_of)
        copy(place, place, col_send.at[0], col_recv.at[slot], col_id(0, 0, 1), d).wait_recv()

    send_set(0, 0, 1, 0)
    send_set(0, 0, 0, 1)
    send_set(0, 0, 0, -1)
    send_col(0, 0, 0, 1, 0)
    send_col(0, 0, 1, 0, 0)
    send_col(0, 0, -1, 0, 0)
    send_col(0, 0, 0, 0, 1)

    def pass_set(step):
        if step == 0:
            wait_set(1, 0)
            send_set(1, 0, 0, 1)
            send_set(1, 0, 0, -1)
            return
        last = step == zs // 2 - 1
        for fy in (0, 1):
            wait_set(fy, -step)
            send_set(fy, -step, 0, 1, 0 if last else None)
            wait_set(fy, step)
            send_set(fy, step, 0, -1, 1 if last else None)

    def pass_col(step):
        if step == 0:
            wait_col(0, 1, 0)
            send_col(0, 1, 1, 0, 0)
            send_col(0, 1, -1, 0, 0)
            send_col(0, 1, 0, 0, 1)
        elif step == 1:
            for fy in (0, 1):
                wait_col(-1, fy, 0)
                send_col(-1, fy, 1, 0, 0, 0)
                send_col(-1, fy, 0, 0, 1)
                wait_col(1, fy, 0)
                send_col(1, fy, -1, 0, 0, 1)
                send_col(1, fy, 0, 0, 1)
        else:
            for fy in (0, 1):
                wait_col(2, fy, 0, 0)
                wait_col(2, fy, 0, 1)
                send_col(2, fy, 0, 0, 1)

    def exchange(src_of, dst, send, recv, along):
        me, size = (d, columns) if along == "dp" else (g, groups)

        def at(o):
            peer = lax.rem(me + o, size)
            where = (g, peer) if along == "dp" else (peer, d)
            return copy(src_of(peer), dst(me), send.at[o], recv.at[o], *where)

        def arrive(o):
            source = lax.rem(me + size - o, size)
            where = (g, source) if along == "dp" else (source, d)
            copy(dst(source), dst(source), send.at[o], recv.at[o], *where).wait_recv()

        return (
            lambda: loop(1, size, lambda o: at(lax.rem(5 * o, size)).start()),
            lambda: loop(1, size, arrive),
            lambda: loop(1, size, lambda o: at(o).wait_send()),
        )

    unit_start, unit_wait, unit_end = exchange(
        lambda peer: unit_t.at[peer], lambda me: cols_t.at[rows_of(me)], unit_send, unit_recv, "group"
    )
    unit_start()
    cols_t[rows_of(g)] = unit_t[g]

    local[0].wait()
    local[1].wait()
    local[3].wait()
    back[...] = jnp.zeros_like(back)

    def project(q, carry):
        squares, along = carry
        p = dot(s_set[rows_of(d)], proj[:, chunk_of(q)])
        both = p * unit_t[q].astype(F32)
        back[...] += dot_t(p.astype(BF16), proj[:, chunk_of(q)])
        for i in range(0, chunk, 128):
            piece = p[:, i : i + 128]
            squares = squares + piece * piece
            along = along + both[:, i : i + 128]
        return squares, along

    zero = jnp.zeros((rows, 128), F32)
    squares, along = lax.fori_loop(0, count, project, (zero, zero))
    norm = jnp.sqrt(jnp.sum(squares, 1, keepdims=True) + EPSILON)
    cosine = jnp.sum(along, 1, keepdims=True)
    inverse = 1.0 / norm

    def split_store(value):
        high = value.astype(BF16)
        pair_rows[0:rows] = high
        pair_rows[rows : 2 * rows] = (value - high.astype(F32)).astype(BF16)

    split_store(back[...] * inverse)
    pass_set(0)

    sub = lax.broadcasted_iota(jnp.int32, (rows, rows), 0)
    lane = lax.broadcasted_iota(jnp.int32, (rows, rows), 1)
    eye = sub == lane

    def to_row(column):
        return jnp.sum(jnp.where(eye, column, 0.0), 0, keepdims=True)

    def to_column(row):
        return jnp.sum(jnp.where(eye, row, 0.0), 1, keepdims=True)

    for one in range(4, 9):
        local[one].wait()

    def teacher_exp(b, total):
        value = jnp.exp(sim_t[:, lanes_of(b)] * INVERSE_TEMP)
        value = jnp.where(jnp.logical_and(eye, b == d), 0.0, value)
        exp_t[b] = value
        return total + value

    total_t = jnp.sum(lax.fori_loop(0, columns, teacher_exp, zero), 1, keepdims=True)
    weight_row = text_weight[...]
    used = hard_count[...]
    facts[0:1, :] = to_row(inverse)
    facts[1:2, :] = to_row(1.0 / total_t)
    facts[2:3, :] = weight_row
    for k in range(HARD):
        facts[3 + k : 4 + k, :] = (
            hard_group[k : k + 1, :] * rows + hard_local[k : k + 1, :]
        ).astype(F32)
        facts[5 + k : 6 + k, :] = (
            jnp.where(used > k, HARD_WEIGHT / used.astype(F32), 0.0) * weight_row
        )
    facts[7:8, :] = jnp.zeros((1, rows), F32)
    facts_set[d] = facts[...]
    facts_col[g] = facts[...]
    fcol_start, fcol_wait, fcol_end = exchange(
        lambda peer: facts, lambda me: facts_col.at[me], fcol_send, fcol_recv, "group"
    )
    fset_start, fset_wait, fset_end = exchange(
        lambda peer: facts, lambda me: facts_set.at[me], fset_send, fset_recv, "dp"
    )
    fcol_start()
    fset_start()
    pass_set(1)
    pass_col(0)

    row_total[...] = zero

    def multiply(block):
        both = dot_t(pair_rows[...], s_set[rows_of(block)])
        sim_s[block] = both[0:rows] + both[rows : 2 * rows]
        s_turned[:, lanes_of(block)] = s_set[rows_of(block)].T

    def finish(block):
        value = sim_s[block] * facts_set[block, 0:1, :]
        grown = jnp.exp(value * INVERSE_TEMP)
        grown = jnp.where(jnp.logical_and(eye, block == d), 0.0, grown)
        sim_s[block] = value
        exp_s[block] = grown
        row_total[...] += grown

    for fy, dz in ((0, 0), (1, 0), (0, -1), (0, 1), (1, -1), (1, 1)):
        multiply(set_id(fy, dz))
    pass_set(2)
    pass_col(1)
    for fy, dz in ((0, -2), (0, 2), (1, -2), (1, 2)):
        multiply(set_id(fy, dz))

    unit_wait()
    fcol_wait()
    numbers = lax.broadcasted_iota(jnp.int32, (rows, 2 * rows), 0).astype(F32)
    step_blocks = 4

    def pick(b):
        queries = cols_t[pl.ds(pl.multiple_of(2 * b * rows, 2 * rows), 2 * rows)]
        first, second = [
            jnp.concatenate([facts_col[2 * b + i, 3 + k : 4 + k, :] for i in (0, 1)], 1)
            for k in range(HARD)
        ]
        sums = [jnp.zeros((1, 2 * rows), F32)] * HARD
        for c in range(0, groups, step_blocks):
            gram = dot_t(cols_t[c * rows : (c + step_blocks) * rows], queries)
            for j in range(step_blocks):
                low = float((c + j) * rows)
                here = jnp.logical_and(first >= low, first < low + rows)
                wanted = jnp.where(here, first, second) - low
                found = jnp.sum(
                    jnp.where(numbers == wanted, gram[j * rows : (j + 1) * rows], 0.0),
                    0,
                    keepdims=True,
                )
                sums[0] = sums[0] + jnp.where(here, found, 0.0)
                sums[1] = sums[1] + jnp.where(here, 0.0, found)
        for k in range(HARD):
            for i in (0, 1):
                part[pl.ds(k * groups + 2 * b + i, 1), :] = sums[k][:, i * rows : (i + 1) * rows]

    loop(0, groups // 4, pick)
    pass_set(3)
    pass_col(2)
    loop(groups // 4, groups // 2, pick)
    part_start, part_wait, part_end = exchange(
        lambda peer: part, lambda me: parts.at[me], part_send, part_recv, "group"
    )
    part_start()
    parts[g] = part[...]
    for fy, dz in ((0, -3), (0, 3), (1, -3), (1, 3)):
        multiply(set_id(fy, dz))
    fset_wait()

    def finish_near(i):
        fy, dz = i // (zs - 1), lax.rem(i, zs - 1) - (zs // 2 - 1)
        finish((yl + fy - 2 * fy * yl) * zs + lax.rem(z + dz + zs, zs))

    loop(0, 2 * (zs - 1), finish_near)
    for dx in range(xs):
        for fy in (0, 1):
            wait_col(dx, fy, 1)

    def cross_pair(b):
        both = dot_t(
            pair_rows[...], s_col[pl.ds(pl.multiple_of(2 * b * rows, 2 * rows), 2 * rows)]
        )
        value = both[0:rows] + both[rows : 2 * rows]
        for i in (0, 1):
            cross_s[2 * b + i] = (
                value[:, i * rows : (i + 1) * rows] * facts_col[2 * b + i, 0:1, :]
            )

    loop(0, groups // 2, cross_pair)
    for fy in (0, 1):
        wait_set(fy, zs // 2, 0)
        wait_set(fy, zs // 2, 1)
        far = set_id(fy, zs // 2)
        multiply(far)
        finish(far)
    total_s = jnp.sum(row_total[...], 1, keepdims=True)
    totals[...] = jnp.broadcast_to(to_row(1.0 / total_s), totals.shape)
    totals_set[d] = totals[...]
    tot_start, tot_wait, tot_end = exchange(
        lambda peer: totals, lambda me: totals_set.at[me], tot_send, tot_recv, "dp"
    )
    tot_start()

    part_wait()
    hard_sum[...] = jnp.sum(parts[...], 0)
    weight = to_column(weight_row)
    own_hard = [to_column(hard_sum[pl.ds(k * groups + g, 1), :]) for k in range(HARD)]
    own_target = [to_column(facts[3 + k : 4 + k, :]) for k in range(HARD)]
    own_entry = [to_column(facts[5 + k : 6 + k, :]) for k in range(HARD)]
    own_ids = sub.astype(F32) + (g * rows).astype(F32)
    lane_ids = lane.astype(F32)

    def hard(b, loss):
        scale = facts_col[b, 0:1, :]
        cross = cross_s[b]
        ids = lane_ids + (b * rows).astype(F32)
        value = jnp.zeros_like(cross)
        for k in range(HARD):
            asked = jnp.where(ids == own_target[k], own_entry[k], 0.0)
            difference = cross - own_hard[k]
            term = asked * difference
            loss = loss + term * difference
            listed = jnp.where(
                facts_col[b, 3 + k : 4 + k, :] == own_ids, facts_col[b, 5 + k : 6 + k, :], 0.0
            )
            value = value + term + listed * (cross - hard_sum[pl.ds(k * groups + b, 1), :])
        h_mat[:, lanes_of(b)] = (2.0 * scale * value).astype(BF16)
        return loss

    hard_loss = lax.fori_loop(0, groups, hard, zero)
    piece = 256 if width >= 256 else width
    for n in range(0, width, piece):
        comb[:, n : n + piece] = dot(h_mat[...], s_col[:, n : n + piece])
    scale_s, scale_t = weight / total_s, weight / total_t

    def pairs(b, carry):
        squares, divergence = carry
        gap = sim_s[b] - sim_t[:, lanes_of(b)]
        their = facts_set[b, 2:3, :]
        grown = exp_t[b]
        sim_s[b] = (2.0 * SIMILARITY_COEF / set_count) * gap * (
            weight + their
        ) + INVERSE_TEMP * (exp_s[b] * scale_s - grown * (scale_t + their * facts_set[b, 1:2, :]))
        return squares + gap * gap, divergence + grown * gap

    squares, divergence = lax.fori_loop(0, columns, pairs, (zero, zero))
    tot_wait()

    def complete(b):
        their = INVERSE_TEMP * facts_set[b, 2:3, :] * totals_set[b, 0:1, :]
        w_mat[:, lanes_of(b)] = (
            (sim_s[b] + exp_s[b] * their) * facts_set[b, 0:1, :]
        ).astype(BF16)

    loop(0, columns, complete)
    for n in range(0, width, piece):
        comb[:, n : n + piece] += dot(w_mat[...], s_set[:, n : n + piece])
    combined = comb[...] * LOSS_SCALE
    inner = jnp.sum(back[...] * combined, 1, keepdims=True) - LOSS_SCALE * weight * cosine
    split_store(
        combined * inverse
        - s_set[rows_of(d)].astype(F32) * (inner * inverse * inverse * inverse)
    )
    thin = chunk // 2
    teacher_scale = LOSS_SCALE * weight * inverse

    def gradient(q):
        both = dot(pair_rows[...], proj[:, chunk_of(q)])
        value = both[0:rows] + both[rows : 2 * rows] - teacher_scale * unit_t[q].astype(F32)
        for h in (0, 1):
            grad[h, q] = value[:, h * thin : (h + 1) * thin].astype(BF16)

    def set_copy(o):
        peer = lax.rem(d + o, columns)
        return copy(
            grad.at[0, peer],
            grad_cols.at[0, rows_of(d)],
            grad_send.at[0, o],
            grad_recv.at[0, o],
            g,
            peer,
        )

    def col_copy(o):
        peer = lax.rem(g + o, groups)
        return copy(
            grad.at[1, peer],
            grad_cols.at[1, rows_of(g)],
            grad_send.at[1, o],
            grad_recv.at[1, o],
            peer,
            d,
        )

    def gradient_step(o):
        turn = lax.rem(5 * o, columns)
        q = lax.rem(d + turn, columns)
        gradient(q)
        apart = lax.rem(q + groups - g, groups)

        @pl.when(apart != 0)
        def send_col_part():
            col_copy(apart).start()

        @pl.when(o != columns)
        def send_set_part():
            set_copy(turn).start()

    loop(1, columns + 1, gradient_step)
    grad_cols[0, rows_of(d)] = grad[0, d]
    grad_cols[1, rows_of(g)] = grad[1, g]

    sim_term = (SIMILARITY_COEF / set_count) * jnp.sum(squares, 1, keepdims=True)
    kl_term = (
        jnp.log(total_s)
        - jnp.log(total_t)
        - INVERSE_TEMP * jnp.sum(divergence, 1, keepdims=True) / total_t
    )
    per_text = weight * (1.0 - cosine * inverse + sim_term + kl_term) + jnp.sum(
        hard_loss, 1, keepdims=True
    )
    loss_tile[...] = jnp.broadcast_to(jnp.sum(per_text, 0, keepdims=True), loss_tile.shape)
    loss_set[d] = loss_tile[...]
    lset_start, lset_wait, lset_end = exchange(
        lambda peer: loss_tile, lambda me: loss_set.at[me], lset_send, lset_recv, "dp"
    )
    lset_start()

    def turn_col(b):
        c_turned[:, lanes_of(b)] = s_col[rows_of(b)].T

    loop(0, groups, turn_col)

    def set_arrive(o):
        source = lax.rem(d + columns - o, columns)
        place = grad_cols.at[0, rows_of(source)]
        copy(place, place, grad_send.at[0, o], grad_recv.at[0, o], g, source).wait_recv()

    def col_arrive(o):
        source = lax.rem(g + groups - o, groups)
        place = grad_cols.at[1, rows_of(source)]
        copy(place, place, grad_send.at[1, o], grad_recv.at[1, o], source, d).wait_recv()

    share = width // groups

    def products(h, turned):
        for n in range(0, width, piece):
            result = dot(turned[n : n + piece, :], grad_cols[h]).astype(BF16)
            for i in range(piece // share):
                within[h, n // share + i] = result[i * share : (i + 1) * share]

    def out_exchange(h, along):
        return exchange(
            lambda peer: within.at[h, peer],
            lambda me: arrived.at[h, me],
            out_send.at[h],
            out_recv.at[h],
            along,
        )

    loop(1, groups, col_arrive)
    products(1, c_turned)
    out1_start, out1_wait, out1_end = out_exchange(1, "dp")
    out1_start()
    arrived[1, d] = within[1, d]

    comb[...] = jnp.zeros_like(comb)

    def student_part(q):
        both = jnp.concatenate([grad[0, q], grad[1, q]], 1)
        comb[...] += dot_t(both, proj[:, chunk_of(q)])

    loop(0, count, student_part)
    student_made[...] = comb[...].astype(BF16)
    student_copy = pltpu.make_async_copy(student_made, student_out, local_sem.at[9])
    student_copy.start()

    for _, one in pending:
        one.wait_send()
    for end in (unit_end, fcol_end, fset_end, part_end, tot_end):
        end()
    lset_wait()
    loss_tile2[...] = jnp.sum(loss_set[...], 0)
    loss_col[g] = loss_tile2[...]
    lcol_start, lcol_wait, lcol_end = exchange(
        lambda peer: loss_tile2, lambda me: loss_col.at[me], lcol_send, lcol_recv, "group"
    )
    lcol_start()

    loop(1, columns, set_arrive)
    products(0, s_turned)
    out0_start, out0_wait, out0_end = out_exchange(0, "group")
    out0_start()
    arrived[0, g] = within[0, g]
    out1_wait()
    mirror_out[...] = jnp.sum(arrived[1].astype(F32), 0)
    mirror = copy(mirror_out, mirror_in, mirror_sem.at[0], mirror_sem.at[1], d, g)

    @pl.when(g != d)
    def send_mirror():
        mirror.start()

    lcol_wait()
    loss_out[0, 0] = jnp.sum(loss_col[...]) * (
        1.0 / (8.0 * 128.0 * rows * groups * columns)
    )
    loop(1, columns, lambda o: set_copy(o).wait_send())
    loop(1, groups, lambda o: col_copy(o).wait_send())
    for end in (lset_end, lcol_end, out1_end):
        end()
    out0_wait()
    projector_out[:, :thin] = jnp.sum(arrived[0].astype(F32), 0)

    @pl.when(g != d)
    def take_mirror():
        mirror.wait()
        projector_out[:, thin:] = mirror_in[...]

    @pl.when(g == d)
    def keep_own():
        projector_out[:, thin:] = mirror_out[...]

    out0_end()
    student_copy.wait()


def local_program(
    student, teacher, teacher_similarity, projector, hard_group, hard_local, hard_count, text_weight
):
    rows, width = student.shape
    groups = lax.axis_size("group")
    columns = lax.axis_size("dp")
    wide = projector.shape[1]
    chunk = wide // groups
    dma = pltpu.SemaphoreType.DMA
    vm = pltpu.VMEM
    texts, col_texts = rows * columns, rows * groups
    scratch = [
        vm((HARD, rows), jnp.int32),
        vm((HARD, rows), jnp.int32),
        vm((1, rows), jnp.int32),
        vm((1, rows), F32),
        vm((rows, width), BF16),
        vm((texts, width), BF16),
        vm((col_texts, width), BF16),
        vm((width, texts), BF16),
        vm((width, col_texts), BF16),
        vm((width, wide), BF16),
        vm((rows, wide), BF16),
        vm((rows, texts), F32),
        vm((groups, rows, chunk), BF16),
        vm((col_texts, chunk), BF16),
        vm((columns, rows, rows), F32),
        vm((columns, rows, rows), F32),
        vm((columns, rows, rows), F32),
        vm((groups, rows, rows), F32),
        vm((rows, rows), F32),
        vm((rows, col_texts), BF16),
        vm((rows, texts), BF16),
        vm((rows, width), F32),
        vm((rows, width), F32),
        vm((2 * rows, width), BF16),
        vm((2, columns, rows, chunk // 2), BF16),
        vm((2, texts, chunk // 2), BF16),
        vm((8, rows), F32),
        vm((columns, 8, rows), F32),
        vm((groups, 8, rows), F32),
        vm((HARD * groups, rows), F32),
        vm((groups, HARD * groups, rows), F32),
        vm((HARD * groups, rows), F32),
        vm((8, rows), F32),
        vm((columns, 8, rows), F32),
        vm((2, groups, width // groups, chunk // 2), BF16),
        vm((2, groups, width // groups, chunk // 2), BF16),
        vm((width // groups, chunk // 2), F32),
        vm((width // groups, chunk // 2), F32),
        vm((8, 128), F32),
        vm((columns, 8, 128), F32),
        vm((8, 128), F32),
        vm((groups, 8, 128), F32),
        dma((10,)),
        dma((2 * columns + 2,)),
        dma((2 * columns,)),
        dma((2 * groups,)),
        dma((2 * groups,)),
    ] + [dma((2, groups) if i in (10, 11, 12, 13) else (groups,)) for i in range(18)] + [dma((2,))]
    anywhere = pl.BlockSpec(memory_space=pl.ANY)
    vmem = pl.BlockSpec(memory_space=pltpu.VMEM)
    loss, student_gradient, projector_gradient = pl.pallas_call(
        functools.partial(kernel, groups, columns),
        out_shape=(
            jax.ShapeDtypeStruct((1, 1), F32),
            jax.ShapeDtypeStruct((rows, width), BF16),
            jax.ShapeDtypeStruct((width // groups, wide // columns), F32),
        ),
        in_specs=[anywhere] * 8,
        out_specs=(pl.BlockSpec(memory_space=pltpu.SMEM), anywhere, vmem),
        scratch_shapes=scratch,
        compiler_params=pltpu.CompilerParams(
            collective_id=0, has_side_effects=True, vmem_limit_bytes=58 * 1024 * 1024
        ),
        cost_estimate=pl.CostEstimate(
            flops=12_000_000_000, bytes_accessed=16_000_000, transcendentals=1_000_000
        ),
    )(
        student,
        teacher,
        teacher_similarity,
        projector,
        hard_group.T,
        hard_local.T,
        hard_count.reshape(1, rows),
        text_weight.reshape(1, rows),
    )
    return loss.reshape(()), student_gradient, projector_gradient


def solution(mesh):
    return jax.shard_map(
        local_program,
        mesh=mesh,
        in_specs=(
            P(("group", "dp"), None),
            P(("group", "dp"), None),
            P(("group", "dp"), None),
            P(),
            P(("group", "dp"), None),
            P(("group", "dp"), None),
            P(("group", "dp")),
            P(("group", "dp")),
        ),
        out_specs=(P(), P(("group", "dp"), None), P("group", "dp")),
        check_vma=False,
    )
```
